32 devices in a mesh: parts: 2 (over y), blk: 4 (over z), users: 2 (over x), sub: 2 (over core).
Axes of the slice: x: 2, y: 2, z: 4, core: 2. Of those that a mesh axis runs over, the one named last changes fastest.
Arguments:
- history: bfloat16 [64, 64, 256], P(('parts', 'blk'), 'users'), parts along dimension 0, may hold values from -400 to 400
- lengths: int32 [64], P(('parts', 'blk')), parts along dimension 0, may hold values from 1 to 64
- item_rows: bfloat16 [12288, 512], P(('parts', 'blk', 'users', 'sub')), parts along dimension 0, may hold values from -6 to 6
- w_query: bfloat16 [512, 256], replicated, may hold values from -0.25 to 0.25
- w_item: bfloat16 [512, 256], replicated, may hold values from -0.25 to 0.25
- w_key: bfloat16 [256, 256], replicated, may hold values from -0.375 to 0.375
- w_value: bfloat16 [256, 256], replicated, may hold values from -0.375 to 0.375
- w_pooled: bfloat16 [256, 128], replicated, may hold values from -0.25 to 0.25
- w_joint: bfloat16 [256, 128], replicated, may hold values from -0.25 to 0.25
- bias_hidden: float32 [128], replicated, may hold values from -3 to 3
- w_task: bfloat16 [128, 8], replicated, may hold values from -0.5 to 0.5
- bias_task: float32 [8], replicated, may hold values from -3 to 3
Outputs:
- logits: float32 [64, 9, 8, 1536], P(('parts', 'blk'), None, None, ('users', 'sub')), parts along dimension 0
The draws below stay inside these ranges and needn't reach their ends.
There are 2 independent parts, one for each index of `parts`. The reference program is written for one: setup_inputs(seed, part) draws one part's arguments, and reference() takes and returns one part's arrays. A program takes and returns all parts, laid end to end along the dimension named above; an argument that names none is the same for every part. Nothing has to cross between parts.
All inputs are finite; a program needn't handle non-finite values.
Results may differ from the reference program's by a relative error of at most 0.011.
Values may be sent and summed in bfloat16 or wider, within the bound.
A program may use at most 64 MiB of HBM per device.

```python
import math
import jax
import jax.numpy as jnp
from jax import lax

DH = 256
DI = 512
HID = 128
TASKS = 8
H = 64
U_DEV = 8
REACH = 4
WIN = 9
USERS = 32
IB = 1536
ITEMS = 6144
N_BLK = 4


def draw_history(key, part):
    entries = jax.random.normal(key, (USERS, H, DH), jnp.float32)
    return jnp.clip(entries, -6.0, 6.0).astype(jnp.bfloat16)


def with_ends(values, rng, low, high):
    shape = values.shape
    place = [jax.random.randint(jax.random.fold_in(rng, axis), (), 0, shape[axis]) for axis in range(len(shape))]
    values = values.at[tuple(place)].set(low)
    longest = shape.index(max(shape))
    place[longest] = (place[longest] + 1) % shape[longest]
    return values.at[tuple(place)].set(high)


def levels(rng, shape, cuts, smallest, largest):
    factor_of, own = 1.0, jax.random.fold_in(rng, 6)
    for dim, shards_of in cuts:
        heights = jnp.exp(jax.random.uniform(jax.random.fold_in(own, dim), (shards_of,), jnp.float32, smallest / len(cuts), largest / len(cuts)))
        factor_of = factor_of * jnp.repeat(heights, shape[dim] // shards_of).reshape([-1 if axis == dim else 1 for axis in range(len(shape))])
    return factor_of


def bell_draw(own_key, shape, width, most, pieces=(), held_as=jnp.bfloat16):
    level = levels(own_key, shape, pieces, -0.22, 0.18) if pieces else 1.0
    values = jax.random.normal(own_key, shape, jnp.float32) * width * level
    return jnp.minimum(jnp.maximum(values, -most), most).astype(held_as)


def setup_inputs(seed: int = 0, part: int = 0) -> dict:
    arg_keys = jax.random.split(jax.random.key(seed), 13)
    part_splits = jax.random.split(jax.random.fold_in(arg_keys[12], part), 13)
    return {
        "history": draw_history(jax.random.fold_in(jax.random.fold_in(arg_keys[12], part), 71), part),
        "lengths": with_ends(jax.random.randint(part_splits[1], (USERS,), 1, H + 1), jax.random.fold_in(part_splits[1], 1), 1, H).astype(jnp.int32),
        "item_rows": bell_draw(part_splits[2], (ITEMS, DI), 1.0, 6.0, ((0, 16),)),
        "w_query": bell_draw(arg_keys[3], (DI, DH), DI ** -0.5, 0.25),
        "w_item": bell_draw(arg_keys[4], (DI, DH), DI ** -0.5, 0.25),
        "w_key": bell_draw(arg_keys[5], (DH, DH), DH ** -0.5, 0.375),
        "w_value": bell_draw(arg_keys[6], (DH, DH), DH ** -0.5, 0.375),
        "w_pooled": bell_draw(arg_keys[7], (DH, HID), (2 * DH) ** -0.5, 0.25),
        "w_joint": bell_draw(arg_keys[8], (DH, HID), (2 * DH) ** -0.5, 0.25),
        "bias_hidden": bell_draw(arg_keys[9], (HID,), 0.5, 3.0, (), jnp.float32),
        "w_task": bell_draw(arg_keys[10], (HID, TASKS), HID ** -0.5, 0.5),
        "bias_task": bell_draw(arg_keys[11], (TASKS,), 0.5, 3.0, (), jnp.float32),
    }


def project(item_rows, w_query, w_item, w_joint, bias_hidden):
    queries = jnp.dot(item_rows, w_query, preferred_element_type=jnp.float32).astype(jnp.bfloat16)
    joined = jnp.dot(item_rows, w_item, preferred_element_type=jnp.float32).astype(jnp.bfloat16)
    item_terms = (jnp.dot(joined, w_joint, preferred_element_type=jnp.float32) + bias_hidden.astype(jnp.float32)).astype(jnp.bfloat16)
    return (queries, item_terms)

def score_pairs(queries, item_terms, key_rows, value_rows, is_valid, w_pooled, w_task, bias_task):
    scale = 1.0 / math.sqrt(queries.shape[-1])
    scores = jnp.einsum('id,utd->uit', queries.astype(jnp.float32), key_rows.astype(jnp.float32)) * scale
    scores = jnp.where(is_valid[:, None, :], scores, -jnp.inf)
    maximum = lax.optimization_barrier(jnp.max(scores, axis=-1, keepdims=True))
    expo = jnp.exp(scores - maximum)
    weights = (expo / lax.optimization_barrier(jnp.sum(expo, axis=-1, keepdims=True))).astype(jnp.bfloat16)
    pooled = jnp.einsum('uit,utd->uid', weights.astype(jnp.float32), value_rows.astype(jnp.float32)).astype(jnp.bfloat16)
    hidden = jnp.einsum('uid,dh->uih', pooled.astype(jnp.float32), w_pooled.astype(jnp.float32)) + item_terms.astype(jnp.float32)[None]
    hidden = jax.nn.relu(hidden).astype(jnp.bfloat16)
    logits = jnp.einsum('uih,hk->uki', hidden.astype(jnp.float32), w_task.astype(jnp.float32))
    return logits + bias_task.astype(jnp.float32)[None, :, None]

def reference(history, lengths, item_rows, w_query, w_item, w_key, w_value, w_pooled, w_joint, bias_hidden, w_task, bias_task):
    queries, item_terms = project(item_rows, w_query, w_item, w_joint, bias_hidden)
    queries = queries.reshape(N_BLK, IB, DH)
    item_terms = item_terms.reshape(N_BLK, IB, HID)
    flat = history.reshape(USERS * H, DH)
    key_rows = jnp.dot(flat, w_key, preferred_element_type=jnp.float32).astype(jnp.bfloat16).reshape(N_BLK, U_DEV, H, DH)
    value_rows = jnp.dot(flat, w_value, preferred_element_type=jnp.float32).astype(jnp.bfloat16).reshape(N_BLK, U_DEV, H, DH)
    is_valid = (jnp.arange(H, dtype=jnp.int32)[None, :] < lengths[:, None]).reshape(N_BLK, U_DEV, H)

    def one_group(index):
        results = []
        for position in range(WIN):
            source = (index + position - REACH) % N_BLK
            results.append(score_pairs(queries[source], item_terms[source], key_rows[index], value_rows[index], is_valid[index], w_pooled, w_task, bias_task))
        return jnp.stack(results, axis=1)
    result = lax.map(one_group, jnp.arange(N_BLK, dtype=jnp.int32))
    return result.reshape(USERS, WIN, TASKS, IB)
```

```python
import functools
import math

import jax
import jax.numpy as jnp
from jax import lax
from jax.experimental import pallas as pl
from jax.experimental.pallas import tpu as pltpu
from jax.sharding import PartitionSpec as P

REACH = 4
WIN = 2 * REACH + 1
LEN_ROWS = 16
F32, BF16 = jnp.float32, jnp.bfloat16


def offsets_of(n_blk):
    if n_blk >= WIN:
        return [k - REACH for k in range(WIN)], list(range(WIN))
    return list(range(n_blk)), [(k - REACH) % n_blk for k in range(WIN)]


def mm(a, b, dims=((1,), (0,))):
    return lax.dot_general(a, b, (dims, ((), ())), preferred_element_type=F32)


def kernel(
    n_blk, n_x, n_sub, hist, lens, items, w_query, w_item, w_key, w_value, w_pooled, w_joint,
    bias_hidden, w_task, bias_task, out, tokens, projected, terms, results,
    z_send, z_recv, x_send, x_recv, c_send, c_recv, r_send, r_recv,
):
    offsets, _ = offsets_of(n_blk)
    own = offsets.index(0)
    order = sorted(range(len(offsets)), key=lambda s: min(offsets[s] % n_blk, -offsets[s] % n_blk))
    users, held, width = hist.shape
    count = users // n_sub
    rows = count * held
    n_items = items.shape[0]
    all_items = n_sub * n_items
    n_hid, n_task = w_task.shape
    me, x, c = lax.axis_index("blk"), lax.axis_index("users"), lax.axis_index("sub")

    def blk_at(distance):
        return lax.rem(me + distance % n_blk, n_blk)

    def x_at(distance):
        return lax.rem(x + distance % n_x, n_x)

    def sub_at(distance):
        return lax.rem(c + distance % n_sub, n_sub)

    tokens[own, x, :rows, :] = hist[pl.ds(c * count, count)].reshape(rows, width)
    row = lax.broadcasted_iota(jnp.int32, (LEN_ROWS, width), 0)
    length_rows = jnp.zeros((LEN_ROWS, width), F32)
    for u in range(count):
        length_rows = jnp.where(row == u, lens[c * count + u].astype(F32), length_rows)
    tokens[own, x, rows:, :] = length_rows.astype(BF16)

    barrier = pltpu.get_barrier_semaphore()
    greeted = 0
    for o in offsets:
        for j in range(n_sub):
            if o != 0 or j != 0:
                target = {"blk": blk_at(o), "sub": sub_at(j)}
                pl.semaphore_signal(barrier, inc=1, device_id=target)
                greeted += 1
    for j in range(1, n_x):
        pl.semaphore_signal(barrier, inc=1, device_id={"users": x_at(j)})
        greeted += 1
    pl.semaphore_wait(barrier, greeted)

    def along_blk(s):
        return pltpu.make_async_remote_copy(
            tokens.at[own, x], tokens.at[s, x], z_send.at[s], z_recv.at[s],
            device_id={"blk": blk_at(offsets[s])},
        )

    def along_x(s, j):
        return pltpu.make_async_remote_copy(
            tokens.at[s, x], tokens.at[s, x], x_send.at[s, j], x_recv.at[s, j],
            device_id={"users": x_at(j)},
        )

    def from_x(s, j):
        there = tokens.at[s, x_at(-j)]
        return pltpu.make_async_remote_copy(
            there, there, x_send.at[s, j], x_recv.at[s, j], device_id={"users": x_at(j)}
        )

    def along_sub(j):
        return pltpu.make_async_remote_copy(
            projected.at[c], projected.at[c], c_send.at[j], c_recv.at[j],
            device_id={"sub": sub_at(j)},
        )

    def from_sub(j):
        there = projected.at[sub_at(-j)]
        return pltpu.make_async_remote_copy(
            there, there, c_send.at[j], c_recv.at[j], device_id={"sub": sub_at(j)}
        )

    def back(s, j):
        source, target = results.at[s, sub_at(j)], out.at[s, c]
        if s == own and j == 0:
            return pltpu.make_async_copy(source, target, r_send.at[s, j])
        return pltpu.make_async_remote_copy(
            source, target, r_send.at[s, j], r_recv.at[s, j],
            device_id={"blk": blk_at(-offsets[s]), "sub": sub_at(j)},
        )

    def from_back(s, j):
        return pltpu.make_async_remote_copy(
            results.at[s, sub_at(j)], out.at[s, sub_at(-j)], r_send.at[s, j], r_recv.at[s, j],
            device_id={"blk": blk_at(-offsets[s]), "sub": sub_at(j)},
        )

    for j in range(1, n_x):
        along_x(own, j).start()
    for s in order[1:]:
        along_blk(s).start()

    item_rows = items[...]
    projected[c, :, :width] = mm(item_rows, w_query[...]).astype(BF16)
    joined = mm(item_rows, w_item[...]).astype(BF16)
    projected[c, :, width:] = (mm(joined, w_joint[...]) + bias_hidden[...][None, :]).astype(BF16)
    for j in range(1, n_sub):
        along_sub(j).start()
    for j in range(1, n_sub):
        from_sub(j).wait_recv()
    for j in range(n_sub):
        terms[:, j * n_items : (j + 1) * n_items] = projected[j, :, width:].astype(F32).T

    head = w_task[...].astype(F32).T
    nothing = jnp.zeros_like(head)
    heads = jnp.concatenate(
        [jnp.concatenate([head, nothing], 1), jnp.concatenate([nothing, head], 1)], 0
    ).astype(BF16)
    row = lax.broadcasted_iota(jnp.int32, (2 * n_task, n_items), 0)
    bias = jnp.zeros((2 * n_task, n_items), F32)
    for t in range(n_task):
        bias = jnp.where((row == t) | (row == t + n_task), bias_task[t], bias)

    factor = math.log2(math.e) / math.sqrt(width)
    place = lax.broadcasted_iota(jnp.int32, (n_x * held, all_items), 0).astype(F32)

    def score(s):
        block = tokens[s, :, :rows, :].reshape(n_x * rows, width)
        keys = mm(block, w_key[...]).astype(BF16)
        values = mm(block, w_value[...]).astype(BF16)
        pooled_values = mm(values, w_pooled[...]).astype(BF16)
        valid_count = tokens[s, 0, rows:, :128].astype(F32)
        queries = projected[:, :, :width].reshape(all_items, width)

        def of_user(array, u):
            return jnp.concatenate(
                [array[p * rows + u * held : p * rows + (u + 1) * held] for p in range(n_x)], 0
            )

        for first in range(0, count, 2):
            hidden = []
            for u in (first, first + 1):
                scores = mm(of_user(keys, u), queries, ((1,), (1,)))
                limit = jnp.concatenate([valid_count[u : u + 1]] * (all_items // 128), 1)
                scores = jnp.where(place < limit, scores, -jnp.inf)
                expo = jnp.exp2((scores - jnp.max(scores, 0, keepdims=True)) * factor)
                weights = (expo * (1.0 / jnp.sum(expo, 0, keepdims=True))).astype(BF16)
                layer = mm(of_user(pooled_values, u), weights, ((0,), (0,))) + terms[...]
                hidden.append(jnp.maximum(layer, 0.0).astype(BF16))
            logits = mm(heads, jnp.concatenate(hidden, 0))
            for j in range(n_sub):
                results[s, j, first * n_task : (first + 2) * n_task, :] = (
                    logits[:, j * n_items : (j + 1) * n_items] + bias
                ).astype(BF16)

    for place_in_order, s in enumerate(order):
        if place_in_order + 1 < len(order):
            later = order[place_in_order + 1]
            along_blk(later).wait_recv()
            for j in range(1, n_x):
                along_x(later, j).start()
        for j in range(1, n_x):
            from_x(s, j).wait_recv()
        score(s)
        for j in range(n_sub):
            back(s, j).start()

    for s in order:
        if s != own:
            along_blk(s).wait_send()
        for j in range(1, n_x):
            along_x(s, j).wait_send()
        for j in range(n_sub):
            if s == own and j == 0:
                back(s, j).wait()
            else:
                back(s, j).wait_send()
                from_back(s, j).wait_recv()
    for j in range(1, n_sub):
        along_sub(j).wait_send()


def shards(
    n_blk, n_x, n_sub, history, lengths, item_rows, w_query, w_item, w_key, w_value, w_pooled,
    w_joint, bias_hidden, w_task, bias_task,
):
    offsets, place_of = offsets_of(n_blk)
    users, held, width = history.shape
    n_items = item_rows.shape[0]
    n_hid, n_task = w_task.shape
    n_slots, count = len(offsets), users // n_sub
    vmem, smem = pl.BlockSpec(memory_space=pltpu.VMEM), pl.BlockSpec(memory_space=pltpu.SMEM)
    dma = pltpu.SemaphoreType.DMA
    by_offset = pl.pallas_call(
        functools.partial(kernel, n_blk, n_x, n_sub),
        out_shape=jax.ShapeDtypeStruct((n_slots, n_sub, count * n_task, n_items), BF16),
        in_specs=[vmem, smem] + [vmem] * 9 + [smem],
        out_specs=pl.BlockSpec(memory_space=pl.ANY),
        scratch_shapes=[
            pltpu.VMEM((n_slots, n_x, count * held + LEN_ROWS, width), BF16),
            pltpu.VMEM((n_sub, n_items, width + n_hid), BF16),
            pltpu.VMEM((n_hid, n_sub * n_items), F32),
            pltpu.VMEM((n_slots, n_sub, count * n_task, n_items), BF16),
            dma((n_slots,)),
            dma((n_slots,)),
            dma((n_slots, n_x)),
            dma((n_slots, n_x)),
            dma((n_sub,)),
            dma((n_sub,)),
            dma((n_slots, n_sub)),
            dma((n_slots, n_sub)),
        ],
        compiler_params=pltpu.CompilerParams(
            collective_id=0, has_side_effects=True, vmem_limit_bytes=40 * 1024 * 1024
        ),
        name="score_users",
    )(
        history, lengths, item_rows, w_query, w_item, w_key, w_value, w_pooled, w_joint,
        bias_hidden, w_task, bias_task,
    )
    by_offset = by_offset.reshape(n_slots, users, n_task, n_items).astype(F32)
    return jnp.stack([by_offset[s] for s in place_of], axis=1)


def solution(mesh):
    placed = (
        P(("parts", "blk"), "users", None),
        P(("parts", "blk")),
        P(("parts", "blk", "users", "sub"), None),
    ) + (P(),) * 9
    sizes = (mesh.shape["blk"], mesh.shape["users"], mesh.shape["sub"])
    return jax.shard_map(
        functools.partial(shards, *sizes),
        mesh=mesh,
        in_specs=placed,
        out_specs=P(("parts", "blk"), None, None, ("users", "sub")),
        check_vma=False,
    )
```

```python
import functools
import math

import jax
import jax.numpy as jnp
from jax import lax
from jax.experimental import pallas as pl
from jax.experimental.pallas import tpu as pltpu
from jax.sharding import PartitionSpec as P

REACH = 4
WIN = 2 * REACH + 1
LEN_ROWS = 16
VMEM_BYTES = 64 * 1024 * 1024
F32, BF16 = jnp.float32, jnp.bfloat16


def offsets_of(n_blk):
    if n_blk >= WIN:
        return [k - REACH for k in range(WIN)], list(range(WIN))
    return list(range(n_blk)), [(k - REACH) % n_blk for k in range(WIN)]


def mm(a, b, dims=((1,), (0,))):
    return lax.dot_general(a, b, (dims, ((), ())), preferred_element_type=F32)


def partner_offsets(n_blk):
    if n_blk >= WIN:
        near = [0] + [sign * d for d in range(1, REACH + 1) for sign in (1, -1)]
        return [near] * n_blk
    return [
        [(m - g) % n_blk for g in sorted(range(n_blk), key=lambda g: (abs(g - m), g))]
        for m in range(n_blk)
    ]


def kernel(
    n_blk, n_x, n_sub, lens, bias_task, hist, *rest
):
    hbm, (out, tokens, *rest) = rest[:9], rest[9:]
    vmem, (projected, queries, terms, results, *sems) = rest[:9], rest[9:]
    z_send, z_recv, x_send, x_recv, c_send, c_recv, r_send, r_recv, load, load_tokens = sems
    items, w_query, w_item, w_joint, bias_hidden, w_key, w_value, w_pooled, w_task = vmem
    n_slots = out.shape[0]
    table = partner_offsets(n_blk)
    lowest = REACH if n_blk >= WIN else 0
    width = hist.shape[1]
    rows = hist.shape[0] // n_sub
    n_task, n_hid = w_task.shape
    count = results.shape[2] // n_task
    held = rows // count
    n_items = items.shape[0]
    all_items = n_sub * n_items
    me, x, c = lax.axis_index("blk"), lax.axis_index("users"), lax.axis_index("sub")

    def offset_at(step):
        found = jnp.int32(0)
        if n_blk >= WIN:
            for i, o in enumerate(table[0]):
                found = jnp.where(step == i, o, found)
        else:
            for m in range(n_blk):
                for i, o in enumerate(table[m]):
                    found = jnp.where((me == m) & (step == i), o, found)
        return found

    def slot_of(o):
        return o + lowest

    def mirror_of(o):
        return REACH - o if n_blk >= WIN else lax.rem(n_blk - o, n_blk)

    def partner_of(o):
        return lax.rem(me - o + n_blk, n_blk)

    def x_at(distance):
        return lax.rem(x + distance % n_x, n_x)

    def sub_at(distance):
        return lax.rem(c + distance % n_sub, n_sub)

    own = lowest
    own_tokens = pltpu.make_async_copy(
        hist.at[pl.ds(c * rows, rows)], tokens.at[own, x, pl.ds(0, rows)], load_tokens
    )
    own_tokens.start()
    loads = [pltpu.make_async_copy(a, b, load.at[i]) for i, (a, b) in enumerate(zip(hbm, vmem))]
    for copy in loads:
        copy.start()

    barrier = pltpu.get_barrier_semaphore()
    greeted = 0
    for o in range(-REACH, REACH + 1) if n_blk >= WIN else range(n_blk):
        for j in range(n_sub):
            if o != 0 or j != 0:
                target = {"blk": lax.rem(me + o % n_blk, n_blk), "sub": sub_at(j)}
                pl.semaphore_signal(barrier, inc=1, device_id=target)
                greeted += 1
    for j in range(1, n_x):
        pl.semaphore_signal(barrier, inc=1, device_id={"users": x_at(j)})
        greeted += 1

    row = lax.broadcasted_iota(jnp.int32, (LEN_ROWS, width), 0)
    length_rows = jnp.zeros((LEN_ROWS, width), F32)
    for u in range(count):
        length_rows = jnp.where(row == u, lens[c * count + u].astype(F32), length_rows)
    tokens[own, x, rows:, :] = length_rows.astype(BF16)
    own_tokens.wait()
    pl.semaphore_wait(barrier, greeted)

    def along_blk(o):
        return pltpu.make_async_remote_copy(
            tokens.at[own, x], tokens.at[mirror_of(o), x],
            z_send.at[mirror_of(o)], z_recv.at[mirror_of(o)],
            device_id={"blk": partner_of(o)},
        )

    def from_blk(o):
        there = tokens.at[slot_of(o), x]
        return pltpu.make_async_remote_copy(
            there, there, z_send.at[slot_of(o)], z_recv.at[slot_of(o)],
            device_id={"blk": partner_of(o)},
        )

    def along_x(s, j):
        return pltpu.make_async_remote_copy(
            tokens.at[s, x], tokens.at[s, x], x_send.at[s, j], x_recv.at[s, j],
            device_id={"users": x_at(j)},
        )

    def from_x(s, j):
        there = tokens.at[s, x_at(-j)]
        return pltpu.make_async_remote_copy(
            there, there, x_send.at[s, j], x_recv.at[s, j], device_id={"users": x_at(j)}
        )

    def along_sub(j):
        return pltpu.make_async_remote_copy(
            projected.at[c], projected.at[c], c_send.at[j], c_recv.at[j],
            device_id={"sub": sub_at(j)},
        )

    def from_sub(j):
        there = projected.at[sub_at(-j)]
        return pltpu.make_async_remote_copy(
            there, there, c_send.at[j], c_recv.at[j], device_id={"sub": sub_at(j)}
        )

    def back(o, j):
        s = slot_of(o)
        return pltpu.make_async_remote_copy(
            results.at[s, sub_at(j)], out.at[s, c], r_send.at[s, j], r_recv.at[s, j],
            device_id={"blk": partner_of(o), "sub": sub_at(j)},
        )

    def from_back(o, j):
        s = slot_of(o)
        there = out.at[s, sub_at(-j)]
        return pltpu.make_async_remote_copy(
            there, there, r_send.at[s, j], r_recv.at[s, j],
            device_id={"blk": partner_of(o), "sub": sub_at(j)},
        )

    own_back = pltpu.make_async_copy(results.at[own, c], out.at[own, c], r_send.at[own, 0])

    for j in range(1, n_x):
        along_x(own, j).start()
    for step in range(1, n_slots):
        along_blk(offset_at(step)).start()

    for copy in loads[:5]:
        copy.wait()
    item_rows = items[...]
    joined = mm(item_rows, w_item[...]).astype(BF16)
    projected[c, width:, :] = (mm(joined, w_joint[...]) + bias_hidden[...]).T.astype(BF16)
    projected[c, :width, :] = mm(item_rows, w_query[...]).T.astype(BF16)
    for j in range(1, n_sub):
        along_sub(j).start()

    for copy in loads[5:]:
        copy.wait()
    head = w_task[...].astype(F32)
    nothing = jnp.zeros_like(head)
    heads = jnp.concatenate(
        [jnp.concatenate([head, nothing], 1), jnp.concatenate([nothing, head], 1)], 0
    ).astype(BF16)
    row = lax.broadcasted_iota(jnp.int32, (2 * n_task, n_items), 0)
    bias = jnp.zeros((2 * n_task, n_items), F32)
    for t in range(n_task):
        bias = jnp.where((row == t) | (row == t + n_task), bias_task[t], bias)

    for j in range(1, n_sub):
        from_sub(j).wait_recv()
    for j in range(n_sub):
        queries[:, j * n_items : (j + 1) * n_items] = projected[j, :width, :]
        terms[:, j * n_items : (j + 1) * n_items] = projected[j, width:, :].astype(F32)

    factor = math.log2(math.e) / math.sqrt(width)
    place = lax.broadcasted_iota(jnp.int32, (n_x * held, 128), 0).astype(F32)

    def score(s):
        block = tokens[s, :, :rows, :].reshape(n_x * rows, width)
        keys = mm(block, w_key[...]).astype(BF16)
        values = mm(block, w_value[...]).astype(BF16)
        pooled_values = mm(values, w_pooled[...]).astype(BF16)
        valid_count = tokens[s, 0, rows:, :128].astype(F32)
        all_scores = mm(keys, queries[...])

        def of_user(array, u):
            return jnp.concatenate(
                [array[p * rows + u * held : p * rows + (u + 1) * held] for p in range(n_x)], 0
            )

        for first in range(0, count, 2):
            hidden = []
            for u in (first, first + 1):
                left_out = jnp.where(place < valid_count[u : u + 1], 0.0, -jnp.inf)
                scores = of_user(all_scores, u) + jnp.concatenate(
                    [left_out] * (all_items // 128), 1
                )
                expo = jnp.exp2((scores - jnp.max(scores, 0, keepdims=True)) * factor)
                weights = (expo * (1.0 / jnp.sum(expo, 0, keepdims=True))).astype(BF16)
                layer = mm(of_user(pooled_values, u), weights, ((0,), (0,))) + terms[...]
                hidden.append(jnp.maximum(layer.astype(BF16), jnp.zeros((), BF16)))
            logits = mm(heads, jnp.concatenate(hidden, 0))
            for j in range(n_sub):
                results[s, j, first * n_task : (first + 2) * n_task, :] = (
                    logits[:, j * n_items : (j + 1) * n_items] + bias
                ).astype(BF16)

    def one_step(step, carry):
        o = offset_at(step)
        s = slot_of(o)

        @pl.when(step + 1 < n_slots)
        def _():
            later = offset_at(step + 1)
            from_blk(later).wait_recv()
            for j in range(1, n_x):
                along_x(slot_of(later), j).start()

        for j in range(1, n_x):
            from_x(s, j).wait_recv()
        score(s)
        for j in range(1, n_sub):
            back(o, j).start()

        @pl.when(step == 0)
        def _():
            own_back.start()

        @pl.when(step > 0)
        def _():
            back(o, 0).start()

        return carry

    lax.fori_loop(0, n_slots, one_step, jnp.int32(0))

    own_back.wait()
    for step in range(n_slots):
        o = offset_at(step)
        if step > 0:
            along_blk(o).wait_send()
        for j in range(1, n_x):
            along_x(slot_of(o), j).wait_send()
        for j in range(0 if step > 0 else 1, n_sub):
            back(o, j).wait_send()
    for s in range(n_slots):
        o = s - lowest
        for j in range(0 if s != own else 1, n_sub):
            from_back(o, j).wait_recv()
    for j in range(1, n_sub):
        along_sub(j).wait_send()


def spread(place_of, by_slot, out, near, wide, load, sems):
    copies = []
    n_slots = by_slot.shape[0]
    loads = [pltpu.make_async_copy(by_slot.at[s], near.at[s], load.at[s]) for s in range(n_slots)]
    for copy in loads:
        copy.start()
    for s in range(n_slots):
        loads[s].wait()
        wide[s] = near[s].astype(F32).reshape(wide.shape[1:])
        for k, slot in enumerate(place_of):
            if slot == s:
                copies.append(pltpu.make_async_copy(wide.at[s], out.at[:, k], sems.at[k]))
                copies[-1].start()
    for copy in copies:
        copy.wait()


def shards(
    n_blk, n_x, n_sub, history, lengths, item_rows, w_query, w_item, w_key, w_value, w_pooled,
    w_joint, bias_hidden, w_task, bias_task,
):
    offsets, place_of = offsets_of(n_blk)
    users, held, width = history.shape
    n_items = item_rows.shape[0]
    n_hid, n_task = w_task.shape
    n_slots, count = len(offsets), users // n_sub
    hbm, smem = pl.BlockSpec(memory_space=pltpu.HBM), pl.BlockSpec(memory_space=pltpu.SMEM)
    dma = pltpu.SemaphoreType.DMA
    held_here = (
        item_rows, w_query, w_item, w_joint, bias_hidden[None], w_key, w_value, w_pooled, w_task.T,
    )
    by_slot = pl.pallas_call(
        functools.partial(kernel, n_blk, n_x, n_sub),
        out_shape=jax.ShapeDtypeStruct((n_slots, n_sub, count * n_task, n_items), BF16),
        in_specs=[smem, smem, hbm] + [hbm] * len(held_here),
        out_specs=pl.BlockSpec(memory_space=pl.ANY),
        scratch_shapes=[
            pltpu.VMEM((n_slots, n_x, count * held + LEN_ROWS, width), BF16),
            *[pltpu.VMEM(a.shape, a.dtype) for a in held_here],
            pltpu.VMEM((n_sub, width + n_hid, n_items), BF16),
            pltpu.VMEM((width, n_sub * n_items), BF16),
            pltpu.VMEM((n_hid, n_sub * n_items), F32),
            pltpu.VMEM((n_slots, n_sub, count * n_task, n_items), BF16),
            dma((n_slots,)),
            dma((n_slots,)),
            dma((n_slots, n_x)),
            dma((n_slots, n_x)),
            dma((n_sub,)),
            dma((n_sub,)),
            dma((n_slots, n_sub)),
            dma((n_slots, n_sub)),
            dma((len(held_here),)),
            dma,
        ],
        compiler_params=pltpu.CompilerParams(
            collective_id=0, has_side_effects=True, vmem_limit_bytes=VMEM_BYTES
        ),
        name="score_users",
    )(lengths, bias_task, history.reshape(users * held, width), *held_here)
    return pl.pallas_call(
        functools.partial(spread, place_of),
        out_shape=jax.ShapeDtypeStruct((users, WIN, n_task, n_items), F32),
        in_specs=[hbm],
        out_specs=pl.BlockSpec(memory_space=pltpu.HBM),
        scratch_shapes=[
            pltpu.VMEM(by_slot.shape, BF16),
            pltpu.VMEM((n_slots, users, n_task, n_items), F32),
            dma((n_slots,)),
            dma((WIN,)),
        ],
        compiler_params=pltpu.CompilerParams(vmem_limit_bytes=VMEM_BYTES),
        name="spread",
    )(by_slot)


def solution(mesh):
    placed = (
        P(("parts", "blk"), "users", None),
        P(("parts", "blk")),
        P(("parts", "blk", "users", "sub"), None),
    ) + (P(),) * 9
    sizes = (mesh.shape["blk"], mesh.shape["users"], mesh.shape["sub"])
    return jax.shard_map(
        functools.partial(shards, *sizes),
        mesh=mesh,
        in_specs=placed,
        out_specs=P(("parts", "blk"), None, None, ("users", "sub")),
        check_vma=False,
    )
```

```python
import functools
import math

import jax
import jax.numpy as jnp
from jax import lax
from jax.experimental import pallas as pl
from jax.experimental.pallas import tpu as pltpu
from jax.sharding import PartitionSpec as P

REACH = 4
WIN = 2 * REACH + 1
LEFT_OUT = 1024.0
VMEM_BYTES = 64 * 1024 * 1024
F32, BF16 = jnp.float32, jnp.bfloat16


def offsets_of(n_blk):
    if n_blk >= WIN:
        return [k - REACH for k in range(WIN)], list(range(WIN))
    return list(range(n_blk)), [(k - REACH) % n_blk for k in range(WIN)]


def mm(a, b, dims=((1,), (0,))):
    return lax.dot_general(a, b, (dims, ((), ())), preferred_element_type=F32)


def partner_offsets(n_blk):
    if n_blk >= WIN:
        near = [0] + [sign * d for d in range(1, REACH + 1) for sign in (1, -1)]
        return [near] * n_blk
    return [
        [(m - g) % n_blk for g in sorted(range(n_blk), key=lambda g: (abs(g - m), g))]
        for m in range(n_blk)
    ]


def kernel(
    n_blk, n_x, n_sub, lens, bias_task, hist, *rest
):
    hbm, (out, tokens, *rest) = rest[:9], rest[9:]
    vmem, (projected, queries, terms, results, *sems) = rest[:9], rest[9:]
    z_send, z_recv, x_send, x_recv, c_send, c_recv, r_send, r_recv, load, load_tokens = sems
    items, w_query, w_item, w_joint, bias_hidden, w_key, w_value, w_pooled, w_task = vmem
    n_slots = out.shape[0]
    table = partner_offsets(n_blk)
    lowest = REACH if n_blk >= WIN else 0
    width = hist.shape[1]
    rows = hist.shape[0] // n_sub
    n_task, n_hid = w_task.shape
    count = results.shape[2] // n_task
    held = rows // count
    n_items = items.shape[0]
    all_items = n_sub * n_items
    me, x, c = lax.axis_index("blk"), lax.axis_index("users"), lax.axis_index("sub")

    def offset_at(step):
        found = jnp.int32(0)
        if n_blk >= WIN:
            for i, o in enumerate(table[0]):
                found = jnp.where(step == i, o, found)
        else:
            for m in range(n_blk):
                for i, o in enumerate(table[m]):
                    found = jnp.where((me == m) & (step == i), o, found)
        return found

    def slot_of(o):
        return o + lowest

    def mirror_of(o):
        return REACH - o if n_blk >= WIN else lax.rem(n_blk - o, n_blk)

    def partner_of(o):
        return lax.rem(me - o + n_blk, n_blk)

    def x_at(distance):
        return lax.rem(x + distance % n_x, n_x)

    def sub_at(distance):
        return lax.rem(c + distance % n_sub, n_sub)

    own = lowest
    own_tokens = pltpu.make_async_copy(
        hist.at[pl.ds(c * rows, rows)], tokens.at[own, x], load_tokens
    )
    own_tokens.start()
    loads = [pltpu.make_async_copy(a, b, load.at[i]) for i, (a, b) in enumerate(zip(hbm, vmem))]
    for copy in loads:
        copy.start()

    barrier = pltpu.get_barrier_semaphore()
    greeted = 0
    for o in range(-REACH, REACH + 1) if n_blk >= WIN else range(n_blk):
        for j in range(n_sub):
            if o != 0 or j != 0:
                target = {"blk": lax.rem(me + o % n_blk, n_blk), "sub": sub_at(j)}
                pl.semaphore_signal(barrier, inc=1, device_id=target)
                greeted += 1
    for j in range(1, n_x):
        pl.semaphore_signal(barrier, inc=1, device_id={"users": x_at(j)})
        greeted += 1

    own_tokens.wait()
    row = lax.broadcasted_iota(jnp.int32, (held, width), 0) + x * held
    for u in range(count):
        mine = tokens[own, x, u * held : (u + 1) * held, :]
        marked = jnp.where(row < lens[c * count + u], mine.astype(F32), LEFT_OUT)
        tokens[own, x, u * held : (u + 1) * held, :] = marked.astype(BF16)
    pl.semaphore_wait(barrier, greeted)

    def along_blk(o):
        return pltpu.make_async_remote_copy(
            tokens.at[own, x], tokens.at[mirror_of(o), x],
            z_send.at[mirror_of(o)], z_recv.at[mirror_of(o)],
            device_id={"blk": partner_of(o)},
        )

    def from_blk(o):
        there = tokens.at[slot_of(o), x]
        return pltpu.make_async_remote_copy(
            there, there, z_send.at[slot_of(o)], z_recv.at[slot_of(o)],
            device_id={"blk": partner_of(o)},
        )

    def along_x(s, j):
        return pltpu.make_async_remote_copy(
            tokens.at[s, x], tokens.at[s, x], x_send.at[s, j], x_recv.at[s, j],
            device_id={"users": x_at(j)},
        )

    def from_x(s, j):
        there = tokens.at[s, x_at(-j)]
        return pltpu.make_async_remote_copy(
            there, there, x_send.at[s, j], x_recv.at[s, j], device_id={"users": x_at(j)}
        )

    def along_sub(j):
        return pltpu.make_async_remote_copy(
            projected.at[c], projected.at[c], c_send.at[j], c_recv.at[j],
            device_id={"sub": sub_at(j)},
        )

    def from_sub(j):
        there = projected.at[sub_at(-j)]
        return pltpu.make_async_remote_copy(
            there, there, c_send.at[j], c_recv.at[j], device_id={"sub": sub_at(j)}
        )

    def back(o, j):
        s = slot_of(o)
        return pltpu.make_async_remote_copy(
            results.at[s, sub_at(j)], out.at[s, c], r_send.at[s, j], r_recv.at[s, j],
            device_id={"blk": partner_of(o), "sub": sub_at(j)},
        )

    def from_back(o, j):
        s = slot_of(o)
        there = out.at[s, sub_at(-j)]
        return pltpu.make_async_remote_copy(
            there, there, r_send.at[s, j], r_recv.at[s, j],
            device_id={"blk": partner_of(o), "sub": sub_at(j)},
        )

    own_back = pltpu.make_async_copy(results.at[own, c], out.at[own, c], r_send.at[own, 0])

    for j in range(1, n_x):
        along_x(own, j).start()
    for step in range(1, n_slots):
        along_blk(offset_at(step)).start()

    for copy in loads[:5]:
        copy.wait()
    item_rows = items[...]
    joined = mm(item_rows, w_item[...]).astype(BF16)
    projected[c, width:, :] = (mm(joined, w_joint[...]) + bias_hidden[...]).T.astype(BF16)
    projected[c, :width, :] = mm(item_rows, w_query[...]).T.astype(BF16)
    for j in range(1, n_sub):
        along_sub(j).start()

    for copy in loads[5:]:
        copy.wait()
    head = w_task[...].astype(F32)
    nothing = jnp.zeros_like(head)
    heads = jnp.concatenate(
        [
            jnp.concatenate([head if v == u else nothing for v in range(count)], 1)
            for u in range(count)
        ],
        0,
    ).astype(BF16)
    row = lax.rem(lax.broadcasted_iota(jnp.int32, (count * n_task, 128), 0), n_task)
    bias = jnp.zeros((count * n_task, 128), F32)
    for t in range(n_task):
        bias = jnp.where(row == t, bias_task[t], bias)
    user = lax.rem(lax.broadcasted_iota(jnp.int32, (n_hid, n_x * rows), 1) // held, count)

    for j in range(1, n_sub):
        from_sub(j).wait_recv()
    for j in range(n_sub):
        queries[:, j * n_items : (j + 1) * n_items] = projected[j, :width, :]
        terms[:, j * n_items : (j + 1) * n_items] = projected[j, width:, :].astype(F32)

    factor = math.log2(math.e) / math.sqrt(width)
    lanes = 256 if all_items % 256 == 0 else 128

    def score(s):
        block = tokens[s].reshape(n_x * rows, width)
        keys = mm(block, w_key[...]).astype(BF16)
        values = mm(block, w_value[...]).astype(BF16)
        pooled_values = mm(values, w_pooled[...]).T
        by_user = jnp.concatenate(
            [jnp.where(user == u, pooled_values, 0.0).astype(BF16) for u in range(count)], 0
        )
        left_out = jnp.where(block[:, :128].astype(F32) > LEFT_OUT / 2, -jnp.inf, 0.0)

        def pieces(array, u):
            at = [p * rows + u * held for p in range(n_x)]
            return jnp.concatenate([array[i : i + held] for i in at], 0)

        for low in range(0, all_items, lanes):
            all_scores = mm(keys, queries[:, low : low + lanes])
            weights = []
            for u in range(count):
                scores = pieces(all_scores, u) + jnp.concatenate(
                    [pieces(left_out, u)] * (lanes // 128), 1
                )
                expo = jnp.exp2((scores - jnp.max(scores, 0, keepdims=True)) * factor)
                weights.append((expo * (1.0 / jnp.sum(expo, 0, keepdims=True))).astype(BF16))
            weights = jnp.concatenate(
                [w[p * held : (p + 1) * held] for p in range(n_x) for w in weights], 0
            )
            layer = mm(by_user, weights) + jnp.concatenate(
                [terms[:, low : low + lanes]] * count, 0
            )
            hidden = jnp.maximum(layer.astype(BF16), jnp.zeros((), BF16))
            logits = mm(heads, hidden)
            for i in range(0, lanes, 128):
                j, at = divmod(low + i, n_items)
                results[s, j, :, at : at + 128] = (logits[:, i : i + 128] + bias).astype(BF16)

    def one_step(step, carry):
        o = offset_at(step)
        s = slot_of(o)

        @pl.when(step + 1 < n_slots)
        def _():
            later = offset_at(step + 1)
            from_blk(later).wait_recv()
            for j in range(1, n_x):
                along_x(slot_of(later), j).start()

        for j in range(1, n_x):
            from_x(s, j).wait_recv()
        score(s)
        for j in range(1, n_sub):
            back(o, j).start()

        @pl.when(step == 0)
        def _():
            own_back.start()

        @pl.when(step > 0)
        def _():
            back(o, 0).start()

        return carry

    lax.fori_loop(0, n_slots, one_step, jnp.int32(0))

    own_back.wait()
    for step in range(n_slots):
        o = offset_at(step)
        if step > 0:
            along_blk(o).wait_send()
        for j in range(1, n_x):
            along_x(slot_of(o), j).wait_send()
        for j in range(0 if step > 0 else 1, n_sub):
            back(o, j).wait_send()
    for s in range(n_slots):
        o = s - lowest
        for j in range(0 if s != own else 1, n_sub):
            from_back(o, j).wait_recv()
    for j in range(1, n_sub):
        along_sub(j).wait_send()


def spread(place_of, by_slot, out, near, wide, load, sems):
    copies = []
    n_slots = by_slot.shape[0]
    loads = [pltpu.make_async_copy(by_slot.at[s], near.at[s], load.at[s]) for s in range(n_slots)]
    for copy in loads:
        copy.start()
    for s in range(n_slots):
        loads[s].wait()
        wide[s] = near[s].astype(F32).reshape(wide.shape[1:])
        for k, slot in enumerate(place_of):
            if slot == s:
                copies.append(pltpu.make_async_copy(wide.at[s], out.at[:, k], sems.at[k]))
                copies[-1].start()
    for copy in copies:
        copy.wait()


def shards(
    n_blk, n_x, n_sub, history, lengths, item_rows, w_query, w_item, w_key, w_value, w_pooled,
    w_joint, bias_hidden, w_task, bias_task,
):
    offsets, place_of = offsets_of(n_blk)
    users, held, width = history.shape
    n_items = item_rows.shape[0]
    n_hid, n_task = w_task.shape
    n_slots, count = len(offsets), users // n_sub
    hbm, smem = pl.BlockSpec(memory_space=pltpu.HBM), pl.BlockSpec(memory_space=pltpu.SMEM)
    dma = pltpu.SemaphoreType.DMA
    held_here = (
        item_rows, w_query, w_item, w_joint, bias_hidden[None], w_key, w_value, w_pooled, w_task.T,
    )
    by_slot = pl.pallas_call(
        functools.partial(kernel, n_blk, n_x, n_sub),
        out_shape=jax.ShapeDtypeStruct((n_slots, n_sub, count * n_task, n_items), BF16),
        in_specs=[smem, smem, hbm] + [hbm] * len(held_here),
        out_specs=pl.BlockSpec(memory_space=pl.ANY),
        scratch_shapes=[
            pltpu.VMEM((n_slots, n_x, count * held, width), BF16),
            *[pltpu.VMEM(a.shape, a.dtype) for a in held_here],
            pltpu.VMEM((n_sub, width + n_hid, n_items), BF16),
            pltpu.VMEM((width, n_sub * n_items), BF16),
            pltpu.VMEM((n_hid, n_sub * n_items), F32),
            pltpu.VMEM((n_slots, n_sub, count * n_task, n_items), BF16),
            dma((n_slots,)),
            dma((n_slots,)),
            dma((n_slots, n_x)),
            dma((n_slots, n_x)),
            dma((n_sub,)),
            dma((n_sub,)),
            dma((n_slots, n_sub)),
            dma((n_slots, n_sub)),
            dma((len(held_here),)),
            dma,
        ],
        compiler_params=pltpu.CompilerParams(
            collective_id=0, has_side_effects=True, vmem_limit_bytes=VMEM_BYTES
        ),
        name="score_users",
    )(lengths, bias_task, history.reshape(users * held, width), *held_here)
    return pl.pallas_call(
        functools.partial(spread, place_of),
        out_shape=jax.ShapeDtypeStruct((users, WIN, n_task, n_items), F32),
        in_specs=[hbm],
        out_specs=pl.BlockSpec(memory_space=pltpu.HBM),
        scratch_shapes=[
            pltpu.VMEM(by_slot.shape, BF16),
            pltpu.VMEM((n_slots, users, n_task, n_items), F32),
            dma((n_slots,)),
            dma((WIN,)),
        ],
        compiler_params=pltpu.CompilerParams(vmem_limit_bytes=VMEM_BYTES),
        name="spread",
    )(by_slot)


def solution(mesh):
    placed = (
        P(("parts", "blk"), "users", None),
        P(("parts", "blk")),
        P(("parts", "blk", "users", "sub"), None),
    ) + (P(),) * 9
    sizes = (mesh.shape["blk"], mesh.shape["users"], mesh.shape["sub"])
    return jax.shard_map(
        functools.partial(shards, *sizes),
        mesh=mesh,
        in_specs=placed,
        out_specs=P(("parts", "blk"), None, None, ("users", "sub")),
        check_vma=False,
    )
```

```python
import functools
import math

import jax
import jax.numpy as jnp
from jax import lax
from jax.experimental import pallas as pl
from jax.experimental.pallas import tpu as pltpu
from jax.sharding import PartitionSpec as P

REACH = 4
WIN = 2 * REACH + 1
PAIRS = 2
LEFT_OUT = 1024.0
VMEM_BYTES = 64 * 1024 * 1024
F32, BF16 = jnp.float32, jnp.bfloat16


def offsets_of(n_blk):
    if n_blk >= WIN:
        return [k - REACH for k in range(WIN)], list(range(WIN))
    return list(range(n_blk)), [(k - REACH) % n_blk for k in range(WIN)]


def mm(a, b, dims=((1,), (0,))):
    return lax.dot_general(a, b, (dims, ((), ())), preferred_element_type=F32)


def steps_of(n_blk):
    ring = n_blk >= WIN
    orders = []
    for m in range(n_blk):
        order = []
        for d in range(REACH + 1 if ring else n_blk):
            for q in range(PAIRS):
                for g in [m] if d == 0 else [m - d, m + d]:
                    if ring:
                        order.append((m - g, q))
                    elif 0 <= g < n_blk:
                        order.append(((m - g) % n_blk, q))
        orders.append(order)
    return orders[:1] * n_blk if ring else orders


def kernel(
    n_blk, n_x, n_sub, lens, bias_task, hist, *rest
):
    hbm, (out, tokens, *rest) = rest[:9], rest[9:]
    vmem, (projected, queries, terms, results, *sems) = rest[:9], rest[9:]
    own_send, z_send, z_recv, x_send, x_recv, c_send, c_recv, r_send, r_recv, load, load_tokens = sems
    items, w_query, w_item, w_joint, bias_hidden, w_key, w_value, w_pooled, w_task = vmem
    n_slots = out.shape[0]
    table = steps_of(n_blk)
    n_steps = n_slots * PAIRS
    ring = n_blk >= WIN
    lowest = REACH if n_blk >= WIN else 0
    width = hist.shape[1]
    rows = tokens.shape[3]
    n_task, n_hid = w_task.shape
    count = results.shape[3] // n_task
    held = rows // count
    n_items = items.shape[0]
    all_items = n_sub * n_items
    me, x, c = lax.axis_index("blk"), lax.axis_index("users"), lax.axis_index("sub")

    def step_at(step):
        o, q = jnp.int32(0), jnp.int32(0)
        for m in range(1 if ring else n_blk):
            for i, entry in enumerate(table[m]):
                here = (step == i) if ring else (me == m) & (step == i)
                o, q = jnp.where(here, entry[0], o), jnp.where(here, entry[1], q)
        return o, q

    def slot_of(o):
        return o + lowest

    def partner_of(o):
        return lax.rem(me - o + n_blk, n_blk)

    def x_at(distance):
        return lax.rem(x + distance % n_x, n_x)

    def sub_at(distance):
        return lax.rem(c + distance % n_sub, n_sub)

    own = lowest
    own_tokens = [
        pltpu.make_async_copy(
            hist.at[pl.ds((c * PAIRS + q) * rows, rows)], tokens.at[own, q, x], load_tokens.at[q]
        )
        for q in range(PAIRS)
    ]
    for copy in own_tokens:
        copy.start()
    loads = [pltpu.make_async_copy(a, b, load.at[i]) for i, (a, b) in enumerate(zip(hbm, vmem))]
    for copy in loads:
        copy.start()

    barrier = pltpu.get_barrier_semaphore()
    greeted = 0
    for o in range(-REACH, REACH + 1) if n_blk >= WIN else range(n_blk):
        for j in range(n_sub):
            if o != 0 or j != 0:
                target = {"blk": lax.rem(me + o % n_blk, n_blk), "sub": sub_at(j)}
                pl.semaphore_signal(barrier, inc=1, device_id=target)
                greeted += 1
    for j in range(1, n_x):
        pl.semaphore_signal(barrier, inc=1, device_id={"users": x_at(j)})
        greeted += 1

    row = lax.broadcasted_iota(jnp.int32, (held, width), 0) + x * held
    for q in range(PAIRS):
        own_tokens[q].wait()
        for u in range(count):
            mine = tokens[own, q, x, u * held : (u + 1) * held, :].astype(F32)
            marked = jnp.where(row < lens[(c * PAIRS + q) * count + u], mine, LEFT_OUT)
            tokens[own, q, x, u * held : (u + 1) * held, :] = marked.astype(BF16)
    pl.semaphore_wait(barrier, greeted)

    def beside(sign):
        there = lax.rem(me + sign + n_blk, n_blk)
        exists = None if ring else (me + 1 < n_blk if sign > 0 else me > 0)

        def seen(o):
            return o + sign + lowest if ring else lax.rem(o + sign + n_blk, n_blk)

        return there, exists, seen

    def own_along_blk(sign, q, act):
        there, exists, seen = beside(sign)
        side = 0 if sign > 0 else 1

        def go():
            act(
                pltpu.make_async_remote_copy(
                    tokens.at[own, q, x], tokens.at[seen(0), q, x],
                    own_send.at[side, q], z_recv.at[seen(0), q], device_id={"blk": there},
                )
            )

        if exists is None:
            go()
        else:
            pl.when(exists)(go)

    def relay(o, q, act):
        s = slot_of(o)
        for sign in (1, -1):
            there, exists, seen = beside(sign)
            if ring:
                onward = (o > 0) & (o < REACH) if sign > 0 else (o < 0) & (o > -REACH)
            else:
                came = partner_of(o) < me if sign > 0 else partner_of(o) > me
                onward = came & exists

            @pl.when(onward)
            def _():
                act(
                    pltpu.make_async_remote_copy(
                        tokens.at[s, q, x], tokens.at[seen(o), q, x],
                        z_send.at[s, q], z_recv.at[seen(o), q], device_id={"blk": there},
                    )
                )

    def from_blk(o, q):
        there = tokens.at[slot_of(o), q, x]
        return pltpu.make_async_remote_copy(
            there, there, z_send.at[slot_of(o), q], z_recv.at[slot_of(o), q],
            device_id={"blk": partner_of(o)},
        )

    def along_x(s, q, j):
        return pltpu.make_async_remote_copy(
            tokens.at[s, q, x], tokens.at[s, q, x], x_send.at[s, q, j], x_recv.at[s, q, j],
            device_id={"users": x_at(j)},
        )

    def from_x(s, q, j):
        there = tokens.at[s, q, x_at(-j)]
        return pltpu.make_async_remote_copy(
            there, there, x_send.at[s, q, j], x_recv.at[s, q, j], device_id={"users": x_at(j)}
        )

    def start(copy):
        copy.start()

    def wait_send(copy):
        copy.wait_send()

    def hand_on(step):
        o, q = step_at(step)
        from_blk(o, q).wait_recv()
        relay(o, q, start)
        for j in range(1, n_x):
            along_x(slot_of(o), q, j).start()

    def along_sub(j):
        return pltpu.make_async_remote_copy(
            projected.at[c], projected.at[c], c_send.at[j], c_recv.at[j],
            device_id={"sub": sub_at(j)},
        )

    def from_sub(j):
        there = projected.at[sub_at(-j)]
        return pltpu.make_async_remote_copy(
            there, there, c_send.at[j], c_recv.at[j], device_id={"sub": sub_at(j)}
        )

    def back(o, q, j):
        s = slot_of(o)
        return pltpu.make_async_remote_copy(
            results.at[s, q, sub_at(j)], out.at[s, c, q], r_send.at[s, q, j], r_recv.at[s, q, j],
            device_id={"blk": partner_of(o), "sub": sub_at(j)},
        )

    def from_back(o, q, j):
        s = slot_of(o)
        there = out.at[s, sub_at(-j), q]
        return pltpu.make_async_remote_copy(
            there, there, r_send.at[s, q, j], r_recv.at[s, q, j],
            device_id={"blk": partner_of(o), "sub": sub_at(j)},
        )

    def own_back(q):
        return pltpu.make_async_copy(
            results.at[own, q, c], out.at[own, c, q], r_send.at[own, q, 0]
        )

    for q in range(PAIRS):
        for sign in (1, -1):
            own_along_blk(sign, q, start)
        for j in range(1, n_x):
            along_x(own, q, j).start()

    for copy in loads[:5]:
        copy.wait()
    item_rows = items[...]
    joined = mm(item_rows, w_item[...]).astype(BF16)
    projected[c, width:, :] = (mm(joined, w_joint[...]) + bias_hidden[...]).T.astype(BF16)
    projected[c, :width, :] = mm(item_rows, w_query[...]).T.astype(BF16)
    for j in range(1, n_sub):
        along_sub(j).start()

    for step in range(PAIRS, min(n_steps, PAIRS + 2)):
        hand_on(step)

    for copy in loads[5:]:
        copy.wait()
    head = w_task[...].astype(F32)
    nothing = jnp.zeros_like(head)
    heads = jnp.concatenate(
        [
            jnp.concatenate([head if v == u else nothing for v in range(count)], 1)
            for u in range(count)
        ],
        0,
    ).astype(BF16)
    row = lax.rem(lax.broadcasted_iota(jnp.int32, (count * n_task, 128), 0), n_task)
    bias = jnp.zeros((count * n_task, 128), F32)
    for t in range(n_task):
        bias = jnp.where(row == t, bias_task[t], bias)
    user = lax.rem(lax.broadcasted_iota(jnp.int32, (n_hid, n_x * rows), 1) // held, count)

    for j in range(1, n_sub):
        from_sub(j).wait_recv()
    for j in range(n_sub):
        queries[:, j * n_items : (j + 1) * n_items] = projected[j, :width, :]
        terms[:, j * n_items : (j + 1) * n_items] = projected[j, width:, :].astype(F32)

    factor = math.log2(math.e) / math.sqrt(width)
    lanes = 256 if all_items % 256 == 0 else 128

    def score(s, q):
        block = tokens[s, q].reshape(n_x * rows, width)
        keys = mm(block, w_key[...]).astype(BF16)
        values = mm(block, w_value[...]).astype(BF16)
        pooled_values = mm(values, w_pooled[...]).T
        by_user = jnp.concatenate(
            [jnp.where(user == u, pooled_values, 0.0).astype(BF16) for u in range(count)], 0
        )
        left_out = jnp.where(block[:, :128].astype(F32) > LEFT_OUT / 2, -jnp.inf, 0.0)

        def pieces(array, u):
            at = [p * rows + u * held for p in range(n_x)]
            return jnp.concatenate([array[i : i + held] for i in at], 0)

        for low in range(0, all_items, lanes):
            all_scores = mm(keys, queries[:, low : low + lanes])
            weights = []
            for u in range(count):
                scores = pieces(all_scores, u) + jnp.concatenate(
                    [pieces(left_out, u)] * (lanes // 128), 1
                )
                expo = jnp.exp2((scores - jnp.max(scores, 0, keepdims=True)) * factor)
                weights.append((expo * (1.0 / jnp.sum(expo, 0, keepdims=True))).astype(BF16))
            weights = jnp.concatenate(
                [w[p * held : (p + 1) * held] for p in range(n_x) for w in weights], 0
            )
            layer = mm(by_user, weights) + jnp.concatenate(
                [terms[:, low : low + lanes]] * count, 0
            )
            hidden = jnp.maximum(layer.astype(BF16), jnp.zeros((), BF16))
            logits = mm(heads, hidden)
            for i in range(0, lanes, 128):
                j, at = divmod(low + i, n_items)
                results[s, q, j, :, at : at + 128] = (logits[:, i : i + 128] + bias).astype(BF16)

    def one_step(step, carry):
        o, q = step_at(step)
        s = slot_of(o)
        ahead = jnp.where(step < 2, step + PAIRS + 2, step + PAIRS + 1)

        @pl.when((step != 2) & (ahead < n_steps))
        def _():
            hand_on(ahead)

        for j in range(1, n_x):
            from_x(s, q, j).wait_recv()
        score(s, q)
        for j in range(1, n_sub):
            back(o, q, j).start()

        @pl.when(step < PAIRS)
        def _():
            own_back(q).start()

        @pl.when(step >= PAIRS)
        def _():
            back(o, q, 0).start()

        return carry

    lax.fori_loop(0, n_steps, one_step, jnp.int32(0))

    for q in range(PAIRS):
        own_back(q).wait()
        for sign in (1, -1):
            own_along_blk(sign, q, wait_send)
    for step in range(n_steps):
        o, q = step_at(step)
        if step >= PAIRS:
            relay(o, q, wait_send)
        for j in range(1, n_x):
            along_x(slot_of(o), q, j).wait_send()
        for j in range(0 if step >= PAIRS else 1, n_sub):
            back(o, q, j).wait_send()
    for s in range(n_slots):
        for q in range(PAIRS):
            for j in range(0 if s != own else 1, n_sub):
                from_back(s - lowest, q, j).wait_recv()
    for j in range(1, n_sub):
        along_sub(j).wait_send()


def spread(place_of, by_slot, out, near, wide, load, sems):
    copies = []
    n_slots = by_slot.shape[0]
    loads = [pltpu.make_async_copy(by_slot.at[s], near.at[s], load.at[s]) for s in range(n_slots)]
    for copy in loads:
        copy.start()
    for s in range(n_slots):
        loads[s].wait()
        wide[s] = near[s].astype(F32).reshape(wide.shape[1:])
        for k, slot in enumerate(place_of):
            if slot == s:
                copies.append(pltpu.make_async_copy(wide.at[s], out.at[:, k], sems.at[k]))
                copies[-1].start()
    for copy in copies:
        copy.wait()


def shards(
    n_blk, n_x, n_sub, history, lengths, item_rows, w_query, w_item, w_key, w_value, w_pooled,
    w_joint, bias_hidden, w_task, bias_task,
):
    offsets, place_of = offsets_of(n_blk)
    users, held, width = history.shape
    n_items = item_rows.shape[0]
    n_hid, n_task = w_task.shape
    n_slots, count = len(offsets), users // n_sub // PAIRS
    hbm, smem = pl.BlockSpec(memory_space=pltpu.HBM), pl.BlockSpec(memory_space=pltpu.SMEM)
    dma = pltpu.SemaphoreType.DMA
    held_here = (
        item_rows, w_query, w_item, w_joint, bias_hidden[None], w_key, w_value, w_pooled, w_task.T,
    )
    by_slot = pl.pallas_call(
        functools.partial(kernel, n_blk, n_x, n_sub),
        out_shape=jax.ShapeDtypeStruct((n_slots, n_sub, PAIRS, count * n_task, n_items), BF16),
        in_specs=[smem, smem, hbm] + [hbm] * len(held_here),
        out_specs=pl.BlockSpec(memory_space=pl.ANY),
        scratch_shapes=[
            pltpu.VMEM((n_slots, PAIRS, n_x, count * held, width), BF16),
            *[pltpu.VMEM(a.shape, a.dtype) for a in held_here],
            pltpu.VMEM((n_sub, width + n_hid, n_items), BF16),
            pltpu.VMEM((width, n_sub * n_items), BF16),
            pltpu.VMEM((n_hid, n_sub * n_items), F32),
            pltpu.VMEM((n_slots, PAIRS, n_sub, count * n_task, n_items), BF16),
            dma((2, PAIRS)),
            dma((n_slots, PAIRS)),
            dma((n_slots, PAIRS)),
            dma((n_slots, PAIRS, n_x)),
            dma((n_slots, PAIRS, n_x)),
            dma((n_sub,)),
            dma((n_sub,)),
            dma((n_slots, PAIRS, n_sub)),
            dma((n_slots, PAIRS, n_sub)),
            dma((len(held_here),)),
            dma((PAIRS,)),
        ],
        compiler_params=pltpu.CompilerParams(
            collective_id=0, has_side_effects=True, vmem_limit_bytes=VMEM_BYTES
        ),
        name="score_users",
    )(lengths, bias_task, history.reshape(users * held, width), *held_here)
    return pl.pallas_call(
        functools.partial(spread, place_of),
        out_shape=jax.ShapeDtypeStruct((users, WIN, n_task, n_items), F32),
        in_specs=[hbm],
        out_specs=pl.BlockSpec(memory_space=pltpu.HBM),
        scratch_shapes=[
            pltpu.VMEM(by_slot.shape, BF16),
            pltpu.VMEM((n_slots, users, n_task, n_items), F32),
            dma((n_slots,)),
            dma((WIN,)),
        ],
        compiler_params=pltpu.CompilerParams(vmem_limit_bytes=VMEM_BYTES),
        name="spread",
    )(by_slot)


def solution(mesh):
    placed = (
        P(("parts", "blk"), "users", None),
        P(("parts", "blk")),
        P(("parts", "blk", "users", "sub"), None),
    ) + (P(),) * 9
    sizes = (mesh.shape["blk"], mesh.shape["users"], mesh.shape["sub"])
    return jax.shard_map(
        functools.partial(shards, *sizes),
        mesh=mesh,
        in_specs=placed,
        out_specs=P(("parts", "blk"), None, None, ("users", "sub")),
        check_vma=False,
    )
```

```python
import functools
import math

import jax
import jax.numpy as jnp
from jax import lax
from jax.experimental import pallas as pl
from jax.experimental.pallas import tpu as pltpu
from jax.sharding import PartitionSpec as P

REACH = 4
WIN = 2 * REACH + 1
LEFT_OUT = 1024.0
VMEM_BYTES = 64 * 1024 * 1024
F32, BF16 = jnp.float32, jnp.bfloat16


def offsets_of(n_blk):
    if n_blk >= WIN:
        return [k - REACH for k in range(WIN)], list(range(WIN))
    return list(range(n_blk)), [(k - REACH) % n_blk for k in range(WIN)]


def mm(a, b, dims=((1,), (0,))):
    return lax.dot_general(a, b, (dims, ((), ())), preferred_element_type=F32)


def partner_offsets(n_blk):
    if n_blk >= WIN:
        near = [0] + [sign * d for d in range(1, REACH + 1) for sign in (1, -1)]
        return [near] * n_blk
    return [
        [(m - g) % n_blk for g in sorted(range(n_blk), key=lambda g: (abs(g - m), g))]
        for m in range(n_blk)
    ]


def kernel(
    n_blk, n_x, n_sub, lens, bias_task, hist, *rest
):
    hbm, (out, tokens, *rest) = rest[:9], rest[9:]
    vmem, (projected, queries, terms, results, *sems) = rest[:9], rest[9:]
    z_send, z_recv, x_send, x_recv, c_send, c_recv, r_send, r_recv, load, load_tokens = sems
    items, w_query, w_item, w_joint, bias_hidden, w_key, w_value, w_pooled, w_task = vmem
    n_slots = out.shape[0]
    table = partner_offsets(n_blk)
    lowest = REACH if n_blk >= WIN else 0
    width = hist.shape[1]
    rows = hist.shape[0] // n_sub
    n_task, n_hid = w_task.shape
    count = results.shape[2] // n_task
    held = rows // count
    n_items = items.shape[0]
    all_items = n_sub * n_items
    me, x, c = lax.axis_index("blk"), lax.axis_index("users"), lax.axis_index("sub")

    def offset_at(step):
        found = jnp.int32(0)
        if n_blk >= WIN:
            for i, o in enumerate(table[0]):
                found = jnp.where(step == i, o, found)
        else:
            for m in range(n_blk):
                for i, o in enumerate(table[m]):
                    found = jnp.where((me == m) & (step == i), o, found)
        return found

    def slot_of(o):
        return o + lowest

    def mirror_of(o):
        return REACH - o if n_blk >= WIN else lax.rem(n_blk - o, n_blk)

    def partner_of(o):
        return lax.rem(me - o + n_blk, n_blk)

    def x_at(distance):
        return lax.rem(x + distance % n_x, n_x)

    def sub_at(distance):
        return lax.rem(c + distance % n_sub, n_sub)

    own = lowest
    own_tokens = pltpu.make_async_copy(
        hist.at[pl.ds(c * rows, rows)], tokens.at[own, x], load_tokens
    )
    own_tokens.start()
    loads = [pltpu.make_async_copy(a, b, load.at[i]) for i, (a, b) in enumerate(zip(hbm, vmem))]
    for copy in loads:
        copy.start()

    barrier = pltpu.get_barrier_semaphore()
    greeted = 0
    for o in range(-REACH, REACH + 1) if n_blk >= WIN else range(n_blk):
        for j in range(n_sub):
            if o != 0 or j != 0:
                target = {"blk": lax.rem(me + o % n_blk, n_blk), "sub": sub_at(j)}
                pl.semaphore_signal(barrier, inc=1, device_id=target)
                greeted += 1
    for j in range(1, n_x):
        pl.semaphore_signal(barrier, inc=1, device_id={"users": x_at(j)})
        greeted += 1

    own_tokens.wait()
    row = lax.broadcasted_iota(jnp.int32, (held, width), 0) + x * held
    for u in range(count):
        mine = tokens[own, x, u * held : (u + 1) * held, :]
        marked = jnp.where(row < lens[c * count + u], mine.astype(F32), LEFT_OUT)
        tokens[own, x, u * held : (u + 1) * held, :] = marked.astype(BF16)
    pl.semaphore_wait(barrier, greeted)

    def along_blk(o):
        return pltpu.make_async_remote_copy(
            tokens.at[own, x], tokens.at[mirror_of(o), x],
            z_send.at[mirror_of(o)], z_recv.at[mirror_of(o)],
            device_id={"blk": partner_of(o)},
        )

    def from_blk(o):
        there = tokens.at[slot_of(o), x]
        return pltpu.make_async_remote_copy(
            there, there, z_send.at[slot_of(o)], z_recv.at[slot_of(o)],
            device_id={"blk": partner_of(o)},
        )

    def along_x(s, j):
        return pltpu.make_async_remote_copy(
            tokens.at[s, x], tokens.at[s, x], x_send.at[s, j], x_recv.at[s, j],
            device_id={"users": x_at(j)},
        )

    def from_x(s, j):
        there = tokens.at[s, x_at(-j)]
        return pltpu.make_async_remote_copy(
            there, there, x_send.at[s, j], x_recv.at[s, j], device_id={"users": x_at(j)}
        )

    def along_sub(j):
        return pltpu.make_async_remote_copy(
            projected.at[c], projected.at[c], c_send.at[j], c_recv.at[j],
            device_id={"sub": sub_at(j)},
        )

    def from_sub(j):
        there = projected.at[sub_at(-j)]
        return pltpu.make_async_remote_copy(
            there, there, c_send.at[j], c_recv.at[j], device_id={"sub": sub_at(j)}
        )

    def back(o, j):
        s = slot_of(o)
        return pltpu.make_async_remote_copy(
            results.at[s, j], out.at[s, c], r_send.at[s, j], r_recv.at[s, j],
            device_id={"blk": partner_of(o), "sub": sub_at(j)},
        )

    def from_back(o, j):
        s = slot_of(o)
        there = out.at[s, sub_at(-j)]
        return pltpu.make_async_remote_copy(
            there, there, r_send.at[s, j], r_recv.at[s, j],
            device_id={"blk": partner_of(o), "sub": sub_at(j)},
        )

    own_back = pltpu.make_async_copy(results.at[own, 0], out.at[own, c], r_send.at[own, 0])

    for j in range(1, n_x):
        along_x(own, j).start()
    for step in range(1, n_slots):
        along_blk(offset_at(step)).start()

    for copy in loads[:5]:
        copy.wait()
    item_rows = items[...]
    joined = mm(item_rows, w_item[...]).astype(BF16)
    projected[c, width:, :] = (mm(joined, w_joint[...]) + bias_hidden[...]).T.astype(BF16)
    projected[c, :width, :] = mm(item_rows, w_query[...]).T.astype(BF16)
    for j in range(1, n_sub):
        along_sub(j).start()

    for copy in loads[5:]:
        copy.wait()
    head = w_task[...].astype(F32)
    nothing = jnp.zeros_like(head)
    heads = jnp.concatenate(
        [
            jnp.concatenate([head if v == u else nothing for v in range(count)], 1)
            for u in range(count)
        ],
        0,
    ).astype(BF16)
    row = lax.rem(lax.broadcasted_iota(jnp.int32, (count * n_task, 128), 0), n_task)
    bias = jnp.zeros((count * n_task, 128), F32)
    for t in range(n_task):
        bias = jnp.where(row == t, bias_task[t], bias)
    user = lax.rem(lax.broadcasted_iota(jnp.int32, (n_hid, n_x * rows), 1) // held, count)

    def take_items(j):
        at = slice(j * n_items, (j + 1) * n_items)
        queries[:, at] = projected[sub_at(j), :width, :]
        terms[:, at] = projected[sub_at(j), width:, :].astype(F32)

    take_items(0)

    factor = math.log2(math.e) / math.sqrt(width)
    lanes = 256 if all_items % 256 == 0 else 128

    def score(s, between):
        block = tokens[s].reshape(n_x * rows, width)
        keys = mm(block, w_key[...]).astype(BF16)
        values = mm(block, w_value[...]).astype(BF16)
        pooled_values = mm(values, w_pooled[...]).T
        by_user = jnp.concatenate(
            [jnp.where(user == u, pooled_values, 0.0).astype(BF16) for u in range(count)], 0
        )
        left_out = jnp.where(block[:, :128].astype(F32) > LEFT_OUT / 2, -jnp.inf, 0.0)

        def pieces(array, u):
            at = [p * rows + u * held for p in range(n_x)]
            return jnp.concatenate([array[i : i + held] for i in at], 0)

        for low in range(0, all_items, lanes):
            between(low)
            all_scores = mm(keys, queries[:, low : low + lanes])
            weights = []
            for u in range(count):
                scores = pieces(all_scores, u) + jnp.concatenate(
                    [pieces(left_out, u)] * (lanes // 128), 1
                )
                expo = jnp.exp2((scores - jnp.max(scores, 0, keepdims=True)) * factor)
                weights.append((expo * (1.0 / jnp.sum(expo, 0, keepdims=True))).astype(BF16))
            weights = jnp.concatenate(
                [w[p * held : (p + 1) * held] for p in range(n_x) for w in weights], 0
            )
            layer = mm(by_user, weights) + jnp.concatenate(
                [terms[:, low : low + lanes]] * count, 0
            )
            hidden = jnp.maximum(layer.astype(BF16), jnp.zeros((), BF16))
            logits = mm(heads, hidden)
            for i in range(0, lanes, 128):
                j, at = divmod(low + i, n_items)
                results[s, j, :, at : at + 128] = (logits[:, i : i + 128] + bias).astype(BF16)

    def hand_on(step):
        later = offset_at(step)
        from_blk(later).wait_recv()
        for j in range(1, n_x):
            along_x(slot_of(later), j).start()

    if n_slots > 1:
        hand_on(1)

    def one_step(step, carry):
        o = offset_at(step)
        s = slot_of(o)

        def between(low):
            if low < n_items < low + lanes or low == n_items:

                @pl.when(step == 0)
                def _():
                    for j in range(1, n_sub):
                        from_sub(j).wait_recv()
                        take_items(j)

            if low + lanes == all_items:

                @pl.when(step + 2 < n_slots)
                def _():
                    hand_on(step + 2)

        for j in range(1, n_x):
            from_x(s, j).wait_recv()
        score(s, between)
        for j in range(1, n_sub):
            back(o, j).start()

        @pl.when(step == 0)
        def _():
            own_back.start()

        @pl.when(step > 0)
        def _():
            back(o, 0).start()

        return carry

    lax.fori_loop(0, n_slots, one_step, jnp.int32(0))

    own_back.wait()
    for step in range(n_slots):
        o = offset_at(step)
        if step > 0:
            along_blk(o).wait_send()
        for j in range(1, n_x):
            along_x(slot_of(o), j).wait_send()
        for j in range(0 if step > 0 else 1, n_sub):
            back(o, j).wait_send()
    for s in range(n_slots):
        o = s - lowest
        for j in range(0 if s != own else 1, n_sub):
            from_back(o, j).wait_recv()
    for j in range(1, n_sub):
        along_sub(j).wait_send()


def spread(place_of, by_slot, out, near, wide, load, sems):
    copies = []
    n_slots = by_slot.shape[0]
    loads = [pltpu.make_async_copy(by_slot.at[s], near.at[s], load.at[s]) for s in range(n_slots)]
    for copy in loads:
        copy.start()
    for s in range(n_slots):
        loads[s].wait()
        wide[s] = near[s].astype(F32).reshape(wide.shape[1:])
        for k, slot in enumerate(place_of):
            if slot == s:
                copies.append(pltpu.make_async_copy(wide.at[s], out.at[:, k], sems.at[k]))
                copies[-1].start()
    for copy in copies:
        copy.wait()


def shards(
    n_blk, n_x, n_sub, history, lengths, item_rows, w_query, w_item, w_key, w_value, w_pooled,
    w_joint, bias_hidden, w_task, bias_task,
):
    offsets, place_of = offsets_of(n_blk)
    users, held, width = history.shape
    n_items = item_rows.shape[0]
    n_hid, n_task = w_task.shape
    n_slots, count = len(offsets), users // n_sub
    hbm, smem = pl.BlockSpec(memory_space=pltpu.HBM), pl.BlockSpec(memory_space=pltpu.SMEM)
    dma = pltpu.SemaphoreType.DMA
    held_here = (
        item_rows, w_query, w_item, w_joint, bias_hidden[None], w_key, w_value, w_pooled, w_task.T,
    )
    by_slot = pl.pallas_call(
        functools.partial(kernel, n_blk, n_x, n_sub),
        out_shape=jax.ShapeDtypeStruct((n_slots, n_sub, count * n_task, n_items), BF16),
        in_specs=[smem, smem, hbm] + [hbm] * len(held_here),
        out_specs=pl.BlockSpec(memory_space=pl.ANY),
        scratch_shapes=[
            pltpu.VMEM((n_slots, n_x, count * held, width), BF16),
            *[pltpu.VMEM(a.shape, a.dtype) for a in held_here],
            pltpu.VMEM((n_sub, width + n_hid, n_items), BF16),
            pltpu.VMEM((width, n_sub * n_items), BF16),
            pltpu.VMEM((n_hid, n_sub * n_items), F32),
            pltpu.VMEM((n_slots, n_sub, count * n_task, n_items), BF16),
            dma((n_slots,)),
            dma((n_slots,)),
            dma((n_slots, n_x)),
            dma((n_slots, n_x)),
            dma((n_sub,)),
            dma((n_sub,)),
            dma((n_slots, n_sub)),
            dma((n_slots, n_sub)),
            dma((len(held_here),)),
            dma,
        ],
        compiler_params=pltpu.CompilerParams(
            collective_id=0, has_side_effects=True, vmem_limit_bytes=VMEM_BYTES
        ),
        name="score_users",
    )(lengths, bias_task, history.reshape(users * held, width), *held_here)
    return pl.pallas_call(
        functools.partial(spread, place_of),
        out_shape=jax.ShapeDtypeStruct((users, WIN, n_task, n_items), F32),
        in_specs=[hbm],
        out_specs=pl.BlockSpec(memory_space=pltpu.HBM),
        scratch_shapes=[
            pltpu.VMEM(by_slot.shape, BF16),
            pltpu.VMEM((n_slots, users, n_task, n_items), F32),
            dma((n_slots,)),
            dma((WIN,)),
        ],
        compiler_params=pltpu.CompilerParams(vmem_limit_bytes=VMEM_BYTES),
        name="spread",
    )(by_slot)


def solution(mesh):
    placed = (
        P(("parts", "blk"), "users", None),
        P(("parts", "blk")),
        P(("parts", "blk", "users", "sub"), None),
    ) + (P(),) * 9
    sizes = (mesh.shape["blk"], mesh.shape["users"], mesh.shape["sub"])
    return jax.shard_map(
        functools.partial(shards, *sizes),
        mesh=mesh,
        in_specs=placed,
        out_specs=P(("parts", "blk"), None, None, ("users", "sub")),
        check_vma=False,
    )
```

```python
import functools
import math

import jax
import jax.numpy as jnp
from jax import lax
from jax.experimental import pallas as pl
from jax.experimental.pallas import tpu as pltpu
from jax.sharding import PartitionSpec as P

REACH = 4
WIN = 2 * REACH + 1
PAIRS = 2
LEFT_OUT = 1024.0
VMEM_BYTES = 64 * 1024 * 1024
F32, BF16 = jnp.float32, jnp.bfloat16


def offsets_of(n_blk):
    if n_blk >= WIN:
        return [k - REACH for k in range(WIN)], list(range(WIN))
    return list(range(n_blk)), [(k - REACH) % n_blk for k in range(WIN)]


def mm(a, b, dims=((1,), (0,))):
    return lax.dot_general(a, b, (dims, ((), ())), preferred_element_type=F32)


def steps_of(n_blk):
    ring = n_blk >= WIN
    orders = []
    for m in range(n_blk):
        order = []
        for d in range(REACH + 1 if ring else n_blk):
            for q in range(PAIRS):
                for g in [m] if d == 0 else [m - d, m + d]:
                    if ring:
                        order.append((m - g, q))
                    elif 0 <= g < n_blk:
                        order.append(((m - g) % n_blk, q))
        orders.append(order)
    return orders[:1] * n_blk if ring else orders


def kernel(
    n_blk, n_x, n_sub, lens, bias_task, hist, *rest
):
    hbm, (out, tokens, *rest) = rest[:9], rest[9:]
    vmem, (projected, queries, terms, results, *sems) = rest[:9], rest[9:]
    own_send, z_send, z_recv, x_send, x_recv, c_send, c_recv, r_send, r_recv, load, load_tokens = sems
    items, w_query, w_item, w_joint, bias_hidden, w_key, w_value, w_pooled, w_task = vmem
    n_slots = out.shape[0]
    table = steps_of(n_blk)
    n_steps = n_slots * PAIRS
    ring = n_blk >= WIN
    lowest = REACH if n_blk >= WIN else 0
    width = hist.shape[1]
    rows = tokens.shape[3]
    n_task, n_hid = w_task.shape
    count = results.shape[2] // n_task // PAIRS
    held = rows // count
    all_users = PAIRS * count
    n_items = items.shape[0]
    all_items = n_sub * n_items
    me, x, c = lax.axis_index("blk"), lax.axis_index("users"), lax.axis_index("sub")

    def step_at(step):
        o, q = jnp.int32(0), jnp.int32(0)
        for m in range(1 if ring else n_blk):
            for i, entry in enumerate(table[m]):
                here = (step == i) if ring else (me == m) & (step == i)
                o, q = jnp.where(here, entry[0], o), jnp.where(here, entry[1], q)
        return o, q

    def offset_at(step):
        found = jnp.int32(0)
        for m in range(1 if ring else n_blk):
            for i, o in enumerate([o for o, q in table[m] if q == 0]):
                here = (step == i) if ring else (me == m) & (step == i)
                found = jnp.where(here, o, found)
        return found

    def slot_of(o):
        return o + lowest

    def partner_of(o):
        return lax.rem(me - o + n_blk, n_blk)

    def x_at(distance):
        return lax.rem(x + distance % n_x, n_x)

    def sub_at(distance):
        return lax.rem(c + distance % n_sub, n_sub)

    own = lowest
    own_tokens = [
        pltpu.make_async_copy(
            hist.at[pl.ds((c * PAIRS + q) * rows, rows)], tokens.at[own, q, x], load_tokens.at[q]
        )
        for q in range(PAIRS)
    ]
    for copy in own_tokens:
        copy.start()
    loads = [pltpu.make_async_copy(a, b, load.at[i]) for i, (a, b) in enumerate(zip(hbm, vmem))]
    for copy in loads:
        copy.start()

    barrier = pltpu.get_barrier_semaphore()
    greeted = 0
    for o in range(-REACH, REACH + 1) if n_blk >= WIN else range(n_blk):
        for j in range(n_sub):
            if o != 0 or j != 0:
                target = {"blk": lax.rem(me + o % n_blk, n_blk), "sub": sub_at(j)}
                pl.semaphore_signal(barrier, inc=1, device_id=target)
                greeted += 1
    for j in range(1, n_x):
        pl.semaphore_signal(barrier, inc=1, device_id={"users": x_at(j)})
        greeted += 1

    row = lax.broadcasted_iota(jnp.int32, (held, width), 0) + x * held
    for q in range(PAIRS):
        own_tokens[q].wait()
        for u in range(count):
            mine = tokens[own, q, x, u * held : (u + 1) * held, :].astype(F32)
            marked = jnp.where(row < lens[(c * PAIRS + q) * count + u], mine, LEFT_OUT)
            tokens[own, q, x, u * held : (u + 1) * held, :] = marked.astype(BF16)
    pl.semaphore_wait(barrier, greeted)

    def beside(sign):
        there = lax.rem(me + sign + n_blk, n_blk)
        exists = None if ring else (me + 1 < n_blk if sign > 0 else me > 0)

        def seen(o):
            return o + sign + lowest if ring else lax.rem(o + sign + n_blk, n_blk)

        return there, exists, seen

    def own_along_blk(sign, q, act):
        there, exists, seen = beside(sign)
        side = 0 if sign > 0 else 1

        def go():
            act(
                pltpu.make_async_remote_copy(
                    tokens.at[own, q, x], tokens.at[seen(0), q, x],
                    own_send.at[side, q], z_recv.at[seen(0), q], device_id={"blk": there},
                )
            )

        if exists is None:
            go()
        else:
            pl.when(exists)(go)

    def relay(o, q, act):
        s = slot_of(o)
        for sign in (1, -1):
            there, exists, seen = beside(sign)
            if ring:
                onward = (o > 0) & (o < REACH) if sign > 0 else (o < 0) & (o > -REACH)
            else:
                came = partner_of(o) < me if sign > 0 else partner_of(o) > me
                onward = came & exists

            @pl.when(onward)
            def _():
                act(
                    pltpu.make_async_remote_copy(
                        tokens.at[s, q, x], tokens.at[seen(o), q, x],
                        z_send.at[s, q], z_recv.at[seen(o), q], device_id={"blk": there},
                    )
                )

    def from_blk(o, q):
        there = tokens.at[slot_of(o), q, x]
        return pltpu.make_async_remote_copy(
            there, there, z_send.at[slot_of(o), q], z_recv.at[slot_of(o), q],
            device_id={"blk": partner_of(o)},
        )

    def along_x(s, q, j):
        return pltpu.make_async_remote_copy(
            tokens.at[s, q, x], tokens.at[s, q, x], x_send.at[s, q, j], x_recv.at[s, q, j],
            device_id={"users": x_at(j)},
        )

    def from_x(s, q, j):
        there = tokens.at[s, q, x_at(-j)]
        return pltpu.make_async_remote_copy(
            there, there, x_send.at[s, q, j], x_recv.at[s, q, j], device_id={"users": x_at(j)}
        )

    def start(copy):
        copy.start()

    def wait_send(copy):
        copy.wait_send()

    def hand_on(step):
        o, q = step_at(step)
        from_blk(o, q).wait_recv()
        relay(o, q, start)
        for j in range(1, n_x):
            along_x(slot_of(o), q, j).start()

    def along_sub(j):
        return pltpu.make_async_remote_copy(
            projected.at[c], projected.at[c], c_send.at[j], c_recv.at[j],
            device_id={"sub": sub_at(j)},
        )

    def from_sub(j):
        there = projected.at[sub_at(-j)]
        return pltpu.make_async_remote_copy(
            there, there, c_send.at[j], c_recv.at[j], device_id={"sub": sub_at(j)}
        )

    def back(o, j):
        s = slot_of(o)
        return pltpu.make_async_remote_copy(
            results.at[s, j], out.at[s, c], r_send.at[s, j], r_recv.at[s, j],
            device_id={"blk": partner_of(o), "sub": sub_at(j)},
        )

    def from_back(o, j):
        s = slot_of(o)
        there = out.at[s, sub_at(-j)]
        return pltpu.make_async_remote_copy(
            there, there, r_send.at[s, j], r_recv.at[s, j],
            device_id={"blk": partner_of(o), "sub": sub_at(j)},
        )

    own_back = pltpu.make_async_copy(results.at[own, 0], out.at[own, c], r_send.at[own, 0])

    for q in range(PAIRS):
        for sign in (1, -1):
            own_along_blk(sign, q, start)
        for j in range(1, n_x):
            along_x(own, q, j).start()

    for copy in loads[:5]:
        copy.wait()
    item_rows = items[...]
    joined = mm(item_rows, w_item[...]).astype(BF16)
    projected[c, width:, :] = (mm(joined, w_joint[...]) + bias_hidden[...]).T.astype(BF16)
    projected[c, :width, :] = mm(item_rows, w_query[...]).T.astype(BF16)
    for j in range(1, n_sub):
        along_sub(j).start()

    for copy in loads[5:]:
        copy.wait()
    head = w_task[...].astype(F32)
    nothing = jnp.zeros_like(head)
    heads = jnp.concatenate(
        [
            jnp.concatenate([head if v == u else nothing for v in range(all_users)], 1)
            for u in range(all_users)
        ],
        0,
    ).astype(BF16)
    row = lax.rem(lax.broadcasted_iota(jnp.int32, (all_users * n_task, 128), 0), n_task)
    bias = jnp.zeros((all_users * n_task, 128), F32)
    for t in range(n_task):
        bias = jnp.where(row == t, bias_task[t], bias)
    token = lax.broadcasted_iota(jnp.int32, (n_hid, PAIRS * n_x * rows), 1)
    user = token // (n_x * rows) * count + lax.rem(token // held, count)

    def take_items(j):
        at = slice(j * n_items, (j + 1) * n_items)
        queries[:, at] = projected[sub_at(j), :width, :]
        terms[:, at] = projected[sub_at(j), width:, :].astype(F32)

    take_items(0)
    for step in range(PAIRS, min(n_steps, PAIRS + 2)):
        hand_on(step)

    factor = math.log2(math.e) / math.sqrt(width)
    lanes = 256 if all_items % 256 == 0 else 128

    def score(s, between):
        block = tokens[s].reshape(PAIRS * n_x * rows, width)
        keys = mm(block, w_key[...]).astype(BF16)
        values = mm(block, w_value[...]).astype(BF16)
        pooled_values = mm(values, w_pooled[...]).T
        by_user = jnp.concatenate(
            [jnp.where(user == u, pooled_values, 0.0).astype(BF16) for u in range(all_users)], 0
        )
        left_out = jnp.where(block[:, :128].astype(F32) > LEFT_OUT / 2, -jnp.inf, 0.0)

        def pieces(array, u):
            q, v = divmod(u, count)
            at = [(q * n_x + p) * rows + v * held for p in range(n_x)]
            return jnp.concatenate([array[i : i + held] for i in at], 0)

        for low in range(0, all_items, lanes):
            between(low)
            all_scores = mm(keys, queries[:, low : low + lanes])
            weights = []
            for u in range(all_users):
                scores = pieces(all_scores, u) + jnp.concatenate(
                    [pieces(left_out, u)] * (lanes // 128), 1
                )
                expo = jnp.exp2((scores - jnp.max(scores, 0, keepdims=True)) * factor)
                weights.append((expo * (1.0 / jnp.sum(expo, 0, keepdims=True))).astype(BF16))
            weights = jnp.concatenate(
                [
                    w[p * held : (p + 1) * held]
                    for q in range(PAIRS)
                    for p in range(n_x)
                    for w in weights[q * count : (q + 1) * count]
                ],
                0,
            )
            layer = mm(by_user, weights) + jnp.concatenate(
                [terms[:, low : low + lanes]] * all_users, 0
            )
            hidden = jnp.maximum(layer.astype(BF16), jnp.zeros((), BF16))
            logits = mm(heads, hidden)
            for i in range(0, lanes, 128):
                j, at = divmod(low + i, n_items)
                results[s, j, :, at : at + 128] = (logits[:, i : i + 128] + bias).astype(BF16)

    def one_step(step, carry):
        o = offset_at(step)
        s = slot_of(o)

        def between(low):
            if low < n_items < low + lanes or low == n_items:

                @pl.when(step == 0)
                def _():
                    for j in range(1, n_sub):
                        from_sub(j).wait_recv()
                        take_items(j)

            for i in range(2):
                if low == (all_items // lanes - 2 + i) * lanes:
                    piece = PAIRS + 2 + 2 * step + i

                    @pl.when(piece < n_steps)
                    def _():
                        hand_on(piece)

        for q in range(PAIRS):
            for j in range(1, n_x):
                from_x(s, q, j).wait_recv()
        score(s, between)
        for j in range(1, n_sub):
            back(o, j).start()

        @pl.when(step == 0)
        def _():
            own_back.start()

        @pl.when(step > 0)
        def _():
            back(o, 0).start()

        return carry

    lax.fori_loop(0, n_slots, one_step, jnp.int32(0))

    own_back.wait()
    for q in range(PAIRS):
        for sign in (1, -1):
            own_along_blk(sign, q, wait_send)
    for step in range(n_steps):
        o, q = step_at(step)
        if step >= PAIRS:
            relay(o, q, wait_send)
        for j in range(1, n_x):
            along_x(slot_of(o), q, j).wait_send()
    for step in range(n_slots):
        for j in range(0 if step > 0 else 1, n_sub):
            back(offset_at(step), j).wait_send()
    for s in range(n_slots):
        for j in range(0 if s != own else 1, n_sub):
            from_back(s - lowest, j).wait_recv()
    for j in range(1, n_sub):
        along_sub(j).wait_send()


def spread(place_of, by_slot, out, near, wide, load, sems):
    copies = []
    n_slots = by_slot.shape[0]
    loads = [pltpu.make_async_copy(by_slot.at[s], near.at[s], load.at[s]) for s in range(n_slots)]
    for copy in loads:
        copy.start()
    for s in range(n_slots):
        loads[s].wait()
        wide[s] = near[s].astype(F32).reshape(wide.shape[1:])
        for k, slot in enumerate(place_of):
            if slot == s:
                copies.append(pltpu.make_async_copy(wide.at[s], out.at[:, k], sems.at[k]))
                copies[-1].start()
    for copy in copies:
        copy.wait()


def shards(
    n_blk, n_x, n_sub, history, lengths, item_rows, w_query, w_item, w_key, w_value, w_pooled,
    w_joint, bias_hidden, w_task, bias_task,
):
    offsets, place_of = offsets_of(n_blk)
    users, held, width = history.shape
    n_items = item_rows.shape[0]
    n_hid, n_task = w_task.shape
    n_slots, count = len(offsets), users // n_sub // PAIRS
    hbm, smem = pl.BlockSpec(memory_space=pltpu.HBM), pl.BlockSpec(memory_space=pltpu.SMEM)
    dma = pltpu.SemaphoreType.DMA
    held_here = (
        item_rows, w_query, w_item, w_joint, bias_hidden[None], w_key, w_value, w_pooled, w_task.T,
    )
    by_slot = pl.pallas_call(
        functools.partial(kernel, n_blk, n_x, n_sub),
        out_shape=jax.ShapeDtypeStruct((n_slots, n_sub, PAIRS * count * n_task, n_items), BF16),
        in_specs=[smem, smem, hbm] + [hbm] * len(held_here),
        out_specs=pl.BlockSpec(memory_space=pl.ANY),
        scratch_shapes=[
            pltpu.VMEM((n_slots, PAIRS, n_x, count * held, width), BF16),
            *[pltpu.VMEM(a.shape, a.dtype) for a in held_here],
            pltpu.VMEM((n_sub, width + n_hid, n_items), BF16),
            pltpu.VMEM((width, n_sub * n_items), BF16),
            pltpu.VMEM((n_hid, n_sub * n_items), F32),
            pltpu.VMEM((n_slots, n_sub, PAIRS * count * n_task, n_items), BF16),
            dma((2, PAIRS)),
            dma((n_slots, PAIRS)),
            dma((n_slots, PAIRS)),
            dma((n_slots, PAIRS, n_x)),
            dma((n_slots, PAIRS, n_x)),
            dma((n_sub,)),
            dma((n_sub,)),
            dma((n_slots, n_sub)),
            dma((n_slots, n_sub)),
            dma((len(held_here),)),
            dma((PAIRS,)),
        ],
        compiler_params=pltpu.CompilerParams(
            collective_id=0, has_side_effects=True, vmem_limit_bytes=VMEM_BYTES
        ),
        name="score_users",
    )(lengths, bias_task, history.reshape(users * held, width), *held_here)
    return pl.pallas_call(
        functools.partial(spread, place_of),
        out_shape=jax.ShapeDtypeStruct((users, WIN, n_task, n_items), F32),
        in_specs=[hbm],
        out_specs=pl.BlockSpec(memory_space=pltpu.HBM),
        scratch_shapes=[
            pltpu.VMEM(by_slot.shape, BF16),
            pltpu.VMEM((n_slots, users, n_task, n_items), F32),
            dma((n_slots,)),
            dma((WIN,)),
        ],
        compiler_params=pltpu.CompilerParams(vmem_limit_bytes=VMEM_BYTES),
        name="spread",
    )(by_slot)


def solution(mesh):
    placed = (
        P(("parts", "blk"), "users", None),
        P(("parts", "blk")),
        P(("parts", "blk", "users", "sub"), None),
    ) + (P(),) * 9
    sizes = (mesh.shape["blk"], mesh.shape["users"], mesh.shape["sub"])
    return jax.shard_map(
        functools.partial(shards, *sizes),
        mesh=mesh,
        in_specs=placed,
        out_specs=P(("parts", "blk"), None, None, ("users", "sub")),
        check_vma=False,
    )
```

```python
import functools
import math

import jax
import jax.numpy as jnp
from jax import lax
from jax.experimental import pallas as pl
from jax.experimental.pallas import tpu as pltpu
from jax.sharding import PartitionSpec as P

REACH = 4
WIN = 2 * REACH + 1
LEFT_OUT = 1024.0
VMEM_BYTES = 64 * 1024 * 1024
F32, BF16 = jnp.float32, jnp.bfloat16


def offsets_of(n_blk):
    if n_blk >= WIN:
        return [k - REACH for k in range(WIN)], list(range(WIN))
    return list(range(n_blk)), [(k - REACH) % n_blk for k in range(WIN)]


def mm(a, b, dims=((1,), (0,))):
    return lax.dot_general(a, b, (dims, ((), ())), preferred_element_type=F32)


def partner_offsets(n_blk):
    if n_blk >= WIN:
        near = [0] + [sign * d for d in range(REACH, 0, -1) for sign in (1, -1)]
        return [near] * n_blk
    return [
        [(m - g) % n_blk for g in sorted(range(n_blk), key=lambda g: (g != m, -abs(g - m), g))]
        for m in range(n_blk)
    ]


def kernel(
    n_blk, n_x, n_sub, lens, bias_task, hist, *rest
):
    hbm, (out, tokens, *rest) = rest[:9], rest[9:]
    vmem, (projected, queries, terms, results, *sems) = rest[:9], rest[9:]
    z_send, z_recv, x_send, x_recv, c_send, c_recv, r_send, r_recv, load, load_tokens = sems
    items, w_query, w_item, w_joint, bias_hidden, w_key, w_value, w_pooled, w_task = vmem
    n_slots = out.shape[0]
    table = partner_offsets(n_blk)
    lowest = REACH if n_blk >= WIN else 0
    width = hist.shape[1]
    rows = hist.shape[0] // n_sub
    n_task, n_hid = w_task.shape
    count = results.shape[2] // n_task
    held = rows // count
    n_items = items.shape[0]
    all_items = n_sub * n_items
    me, x, c = lax.axis_index("blk"), lax.axis_index("users"), lax.axis_index("sub")

    def offset_at(step):
        found = jnp.int32(0)
        if n_blk >= WIN:
            for i, o in enumerate(table[0]):
                found = jnp.where(step == i, o, found)
        else:
            for m in range(n_blk):
                for i, o in enumerate(table[m]):
                    found = jnp.where((me == m) & (step == i), o, found)
        return found

    def slot_of(o):
        return o + lowest

    def mirror_of(o):
        return REACH - o if n_blk >= WIN else lax.rem(n_blk - o, n_blk)

    def partner_of(o):
        return lax.rem(me - o + n_blk, n_blk)

    def x_at(distance):
        return lax.rem(x + distance % n_x, n_x)

    def sub_at(distance):
        return lax.rem(c + distance % n_sub, n_sub)

    own = lowest
    own_tokens = pltpu.make_async_copy(
        hist.at[pl.ds(c * rows, rows)], tokens.at[own, x], load_tokens
    )
    own_tokens.start()
    loads = [pltpu.make_async_copy(a, b, load.at[i]) for i, (a, b) in enumerate(zip(hbm, vmem))]
    for copy in loads:
        copy.start()

    barrier = pltpu.get_barrier_semaphore()
    greeted = 0
    for o in range(-REACH, REACH + 1) if n_blk >= WIN else range(n_blk):
        for j in range(n_sub):
            if o != 0 or j != 0:
                target = {"blk": lax.rem(me + o % n_blk, n_blk), "sub": sub_at(j)}
                pl.semaphore_signal(barrier, inc=1, device_id=target)
                greeted += 1
    for j in range(1, n_x):
        pl.semaphore_signal(barrier, inc=1, device_id={"users": x_at(j)})
        greeted += 1

    own_tokens.wait()
    row = lax.broadcasted_iota(jnp.int32, (held, width), 0) + x * held
    for u in range(count):
        mine = tokens[own, x, u * held : (u + 1) * held, :]
        marked = jnp.where(row < lens[c * count + u], mine.astype(F32), LEFT_OUT)
        tokens[own, x, u * held : (u + 1) * held, :] = marked.astype(BF16)
    pl.semaphore_wait(barrier, greeted)

    def along_blk(o):
        return pltpu.make_async_remote_copy(
            tokens.at[own, x], tokens.at[mirror_of(o), x],
            z_send.at[mirror_of(o)], z_recv.at[mirror_of(o)],
            device_id={"blk": partner_of(o)},
        )

    def from_blk(o):
        there = tokens.at[slot_of(o), x]
        return pltpu.make_async_remote_copy(
            there, there, z_send.at[slot_of(o)], z_recv.at[slot_of(o)],
            device_id={"blk": partner_of(o)},
        )

    def along_x(s, j):
        return pltpu.make_async_remote_copy(
            tokens.at[s, x], tokens.at[s, x], x_send.at[s, j], x_recv.at[s, j],
            device_id={"users": x_at(j)},
        )

    def from_x(s, j):
        there = tokens.at[s, x_at(-j)]
        return pltpu.make_async_remote_copy(
            there, there, x_send.at[s, j], x_recv.at[s, j], device_id={"users": x_at(j)}
        )

    def along_sub(j):
        return pltpu.make_async_remote_copy(
            projected.at[c], projected.at[c], c_send.at[j], c_recv.at[j],
            device_id={"sub": sub_at(j)},
        )

    def from_sub(j):
        there = projected.at[sub_at(-j)]
        return pltpu.make_async_remote_copy(
            there, there, c_send.at[j], c_recv.at[j], device_id={"sub": sub_at(j)}
        )

    def back(o, j):
        s = slot_of(o)
        return pltpu.make_async_remote_copy(
            results.at[s, sub_at(j)], out.at[s, c], r_send.at[s, j], r_recv.at[s, j],
            device_id={"blk": partner_of(o), "sub": sub_at(j)},
        )

    def from_back(o, j):
        s = slot_of(o)
        there = out.at[s, sub_at(-j)]
        return pltpu.make_async_remote_copy(
            there, there, r_send.at[s, j], r_recv.at[s, j],
            device_id={"blk": partner_of(o), "sub": sub_at(j)},
        )

    own_back = pltpu.make_async_copy(results.at[own, c], out.at[own, c], r_send.at[own, 0])

    for j in range(1, n_x):
        along_x(own, j).start()
    for step in range(1, n_slots):
        along_blk(offset_at(step)).start()

    for copy in loads[:5]:
        copy.wait()
    item_rows = items[...]
    joined = mm(item_rows, w_item[...]).astype(BF16)
    projected[c, width:, :] = (mm(joined, w_joint[...]) + bias_hidden[...]).T.astype(BF16)
    projected[c, :width, :] = mm(item_rows, w_query[...]).T.astype(BF16)
    for j in range(1, n_sub):
        along_sub(j).start()

    for copy in loads[5:]:
        copy.wait()
    head = w_task[...].astype(F32)
    nothing = jnp.zeros_like(head)
    heads = jnp.concatenate(
        [
            jnp.concatenate([head if v == u else nothing for v in range(count)], 1)
            for u in range(count)
        ],
        0,
    ).astype(BF16)
    row = lax.rem(lax.broadcasted_iota(jnp.int32, (count * n_task, 128), 0), n_task)
    bias = jnp.zeros((count * n_task, 128), F32)
    for t in range(n_task):
        bias = jnp.where(row == t, bias_task[t], bias)
    user = lax.rem(lax.broadcasted_iota(jnp.int32, (n_hid, n_x * rows), 1) // held, count)

    for j in range(1, n_sub):
        from_sub(j).wait_recv()
    for j in range(n_sub):
        queries[:, j * n_items : (j + 1) * n_items] = projected[j, :width, :]
        terms[:, j * n_items : (j + 1) * n_items] = projected[j, width:, :].astype(F32)

    factor = math.log2(math.e) / math.sqrt(width)
    lanes = 256 if all_items % 256 == 0 else 128

    def score(s):
        block = tokens[s].reshape(n_x * rows, width)
        keys = mm(block, w_key[...]).astype(BF16)
        values = mm(block, w_value[...]).astype(BF16)
        pooled_values = mm(values, w_pooled[...]).T
        by_user = jnp.concatenate(
            [jnp.where(user == u, pooled_values, 0.0).astype(BF16) for u in range(count)], 0
        )
        left_out = jnp.where(block[:, :128].astype(F32) > LEFT_OUT / 2, -jnp.inf, 0.0)

        def pieces(array, u):
            at = [p * rows + u * held for p in range(n_x)]
            return jnp.concatenate([array[i : i + held] for i in at], 0)

        for low in range(0, all_items, lanes):
            all_scores = mm(keys, queries[:, low : low + lanes])
            weights = []
            for u in range(count):
                scores = pieces(all_scores, u) + jnp.concatenate(
                    [pieces(left_out, u)] * (lanes // 128), 1
                )
                expo = jnp.exp2((scores - jnp.max(scores, 0, keepdims=True)) * factor)
                weights.append((expo * (1.0 / jnp.sum(expo, 0, keepdims=True))).astype(BF16))
            weights = jnp.concatenate(
                [w[p * held : (p + 1) * held] for p in range(n_x) for w in weights], 0
            )
            layer = mm(by_user, weights) + jnp.concatenate(
                [terms[:, low : low + lanes]] * count, 0
            )
            hidden = jnp.maximum(layer.astype(BF16), jnp.zeros((), BF16))
            logits = mm(heads, hidden)
            for i in range(0, lanes, 128):
                j, at = divmod(low + i, n_items)
                results[s, j, :, at : at + 128] = (logits[:, i : i + 128] + bias).astype(BF16)

    def one_step(step, carry):
        o = offset_at(step)
        s = slot_of(o)

        @pl.when(step + 1 < n_slots)
        def _():
            later = offset_at(step + 1)
            from_blk(later).wait_recv()
            for j in range(1, n_x):
                along_x(slot_of(later), j).start()

        for j in range(1, n_x):
            from_x(s, j).wait_recv()
        score(s)
        for j in range(1, n_sub):
            back(o, j).start()

        @pl.when(step == 0)
        def _():
            own_back.start()

        @pl.when(step > 0)
        def _():
            back(o, 0).start()

        return carry

    lax.fori_loop(0, n_slots, one_step, jnp.int32(0))

    own_back.wait()
    for step in range(n_slots):
        o = offset_at(step)
        if step > 0:
            along_blk(o).wait_send()
        for j in range(1, n_x):
            along_x(slot_of(o), j).wait_send()
        for j in range(0 if step > 0 else 1, n_sub):
            back(o, j).wait_send()
    for s in range(n_slots):
        o = s - lowest
        for j in range(0 if s != own else 1, n_sub):
            from_back(o, j).wait_recv()
    for j in range(1, n_sub):
        along_sub(j).wait_send()


def spread(place_of, by_slot, out, near, wide, load, sems):
    copies = []
    n_slots = by_slot.shape[0]
    loads = [pltpu.make_async_copy(by_slot.at[s], near.at[s], load.at[s]) for s in range(n_slots)]
    for copy in loads:
        copy.start()
    for s in range(n_slots):
        loads[s].wait()
        wide[s] = near[s].astype(F32).reshape(wide.shape[1:])
        for k, slot in enumerate(place_of):
            if slot == s:
                copies.append(pltpu.make_async_copy(wide.at[s], out.at[:, k], sems.at[k]))
                copies[-1].start()
    for copy in copies:
        copy.wait()


def shards(
    n_blk, n_x, n_sub, history, lengths, item_rows, w_query, w_item, w_key, w_value, w_pooled,
    w_joint, bias_hidden, w_task, bias_task,
):
    offsets, place_of = offsets_of(n_blk)
    users, held, width = history.shape
    n_items = item_rows.shape[0]
    n_hid, n_task = w_task.shape
    n_slots, count = len(offsets), users // n_sub
    hbm, smem = pl.BlockSpec(memory_space=pltpu.HBM), pl.BlockSpec(memory_space=pltpu.SMEM)
    dma = pltpu.SemaphoreType.DMA
    held_here = (
        item_rows, w_query, w_item, w_joint, bias_hidden[None], w_key, w_value, w_pooled, w_task.T,
    )
    by_slot = pl.pallas_call(
        functools.partial(kernel, n_blk, n_x, n_sub),
        out_shape=jax.ShapeDtypeStruct((n_slots, n_sub, count * n_task, n_items), BF16),
        in_specs=[smem, smem, hbm] + [hbm] * len(held_here),
        out_specs=pl.BlockSpec(memory_space=pl.ANY),
        scratch_shapes=[
            pltpu.VMEM((n_slots, n_x, count * held, width), BF16),
            *[pltpu.VMEM(a.shape, a.dtype) for a in held_here],
            pltpu.VMEM((n_sub, width + n_hid, n_items), BF16),
            pltpu.VMEM((width, n_sub * n_items), BF16),
            pltpu.VMEM((n_hid, n_sub * n_items), F32),
            pltpu.VMEM((n_slots, n_sub, count * n_task, n_items), BF16),
            dma((n_slots,)),
            dma((n_slots,)),
            dma((n_slots, n_x)),
            dma((n_slots, n_x)),
            dma((n_sub,)),
            dma((n_sub,)),
            dma((n_slots, n_sub)),
            dma((n_slots, n_sub)),
            dma((len(held_here),)),
            dma,
        ],
        compiler_params=pltpu.CompilerParams(
            collective_id=0, has_side_effects=True, vmem_limit_bytes=VMEM_BYTES
        ),
        name="score_users",
    )(lengths, bias_task, history.reshape(users * held, width), *held_here)
    return pl.pallas_call(
        functools.partial(spread, place_of),
        out_shape=jax.ShapeDtypeStruct((users, WIN, n_task, n_items), F32),
        in_specs=[hbm],
        out_specs=pl.BlockSpec(memory_space=pltpu.HBM),
        scratch_shapes=[
            pltpu.VMEM(by_slot.shape, BF16),
            pltpu.VMEM((n_slots, users, n_task, n_items), F32),
            dma((n_slots,)),
            dma((WIN,)),
        ],
        compiler_params=pltpu.CompilerParams(vmem_limit_bytes=VMEM_BYTES),
        name="spread",
    )(by_slot)


def solution(mesh):
    placed = (
        P(("parts", "blk"), "users", None),
        P(("parts", "blk")),
        P(("parts", "blk", "users", "sub"), None),
    ) + (P(),) * 9
    sizes = (mesh.shape["blk"], mesh.shape["users"], mesh.shape["sub"])
    return jax.shard_map(
        functools.partial(shards, *sizes),
        mesh=mesh,
        in_specs=placed,
        out_specs=P(("parts", "blk"), None, None, ("users", "sub")),
        check_vma=False,
    )
```
